32 devices in a mesh: src: 8 (over y, x, core), rcv: 4 (over z).
Axes of the slice: x: 2, y: 2, z: 4, core: 2. Of those that a mesh axis runs over, the one named last changes fastest.
Arguments:
- records: float32 [256, 20480], P(('rcv', 'src')), may hold values from -500 to 500
- starts: int32 [2], replicated, may hold values from 0 to 10180, as said below
- block_mask: int32 [4, 4, 8], P('rcv', None, 'src'), may hold values from 0 to 1, as said below
Outputs:
- stacked: bfloat16 [256, 4, 8, 8, 128], P('rcv', None, 'src')
The draws below stay inside these ranges and needn't reach their ends.
Inputs may be any that keep to these rules, and one draw needn't show every extreme that they name: Some window starts at 10180. block_mask[a, b, c] is 0 wherever b < a.
All inputs are finite; a program needn't handle non-finite values.
Results may differ from the reference program's by a relative error of at most 0.0065.
Values may be sent and summed in bfloat16 or wider, within the bound.
A program may use at most 192 MiB of HBM per device.

```python
import math
import jax
import jax.numpy as jnp
from jax import lax

CH_DEV = 8
WINDOWS = 2
DEC = 5
KSEG = 13
NT = 2048
FB = 512
HALF = 64
LAGS = 128
TAPS = 65
F = 1024
RAW = 10300
REC = 20480
BLOCK = 64
BLOCKS = 4
SUBS = 8
CHANNELS = 256


def draw_records(key, part):
    key = jax.random.fold_in(key, 5)
    subkeys = jax.random.split(key, 6)
    tone_count = 4
    noise = jnp.clip(jax.random.normal(subkeys[0], (CHANNELS, REC), jnp.float32), -5.0, 5.0)
    channel_gain = jnp.exp(jax.random.uniform(subkeys[1], (CHANNELS, 1), jnp.float32, 0.0, math.log(10.0)))
    tone_bins = jax.random.randint(subkeys[2], (CHANNELS, tone_count), REC // 400, REC // 20)
    offsets = jax.random.randint(subkeys[3], (CHANNELS, tone_count), 0, REC)
    tone_level = jax.random.uniform(subkeys[4], (CHANNELS, tone_count), jnp.float32, 0.5, 2.0)
    drift = jax.random.uniform(subkeys[5], (CHANNELS, 1), jnp.float32, -math.pi, math.pi)
    sample_ids = jnp.arange(REC, dtype=jnp.int32)[None, :]
    signal = noise
    for tone in range(tone_count):
        phase_index = (tone_bins[:, tone:tone + 1] * sample_ids + offsets[:, tone:tone + 1]) % REC
        signal = signal + tone_level[:, tone:tone + 1] * jnp.sin(2.0 * math.pi / REC * phase_index.astype(jnp.float32))
    slow_index = 3 * sample_ids % REC
    envelope = jnp.exp(0.8 * jnp.sin(2.0 * math.pi / REC * slow_index.astype(jnp.float32) + drift))
    return (channel_gain * envelope * signal).astype(jnp.float32)


def draw_starts(key, part):
    key = jax.random.fold_in(key, 7)
    subkeys = jax.random.split(key, 2)
    latest = REC - RAW
    chosen_starts = jax.random.randint(subkeys[0], (WINDOWS,), 0, latest + 1)
    chosen = jax.random.randint(subkeys[1], (), 0, WINDOWS)
    window_ids = jnp.arange(WINDOWS)
    chosen_starts = jnp.where(window_ids == chosen, latest, chosen_starts)
    return chosen_starts.astype(jnp.int32)


def draw_block_mask(key, part):
    key = jax.random.fold_in(key, 11)
    chosen = jax.random.randint(key, (BLOCKS, BLOCKS, SUBS), 0, 4)
    source_ids = jnp.arange(BLOCKS)[:, None, None]
    receiver_ids = jnp.arange(BLOCKS)[None, :, None]
    return jnp.where((receiver_ids >= source_ids) & (chosen > 0), 1, 0).astype(jnp.int32)


def setup_inputs(seed: int = 0) -> dict:
    key_of = jax.random.split(jax.random.key(seed), 4)
    records = draw_records(jax.random.fold_in(key_of[3], 71), 0)
    starts = draw_starts(jax.random.fold_in(key_of[3], 71), 0)
    block_mask = draw_block_mask(jax.random.fold_in(key_of[3], 71), 0)
    return {"records": records, "starts": starts, "block_mask": block_mask}


eps_power = 1e-06

def lowpass():
    tap_index = jnp.arange(TAPS, dtype=jnp.float32)
    centre = (TAPS - 1) / 2.0
    taper = 0.5 - 0.5 * jnp.cos(2.0 * math.pi * (tap_index + 1.0) / (TAPS + 1.0))
    return jnp.sinc((tap_index - centre) / DEC) * taper / DEC

def decimate(windows):
    taps_kernel = lowpass()
    frames = windows.reshape(windows.shape[0], windows.shape[1], NT + KSEG - 1, DEC)
    phases = jnp.swapaxes(frames, 2, 3)
    traces = jnp.zeros((windows.shape[0], windows.shape[1], NT), jnp.float32)
    for segment in range(KSEG):
        weights = taps_kernel[segment * DEC:(segment + 1) * DEC]
        traces = traces + lax.optimization_barrier(jnp.sum(phases[:, :, :, segment:segment + NT] * weights[:, None], axis=2))
    return traces

def smoother(bins, band, reach):
    source_bins = jnp.arange(bins, dtype=jnp.int32)[:, None]
    target_bins = jnp.arange(band, dtype=jnp.int32)[None, :]
    inside = jnp.abs(source_bins - target_bins) <= reach
    lowest = jnp.maximum(target_bins - reach, 0)
    highest = jnp.minimum(target_bins + reach, bins - 1)
    counted = (highest - lowest + 1).astype(jnp.float32)
    return jnp.where(inside, 1.0, 0.0).astype(jnp.float32) / counted

def finish(real_part, imag_part, window_count, channel_count):
    power = real_part * real_part + imag_part * imag_part
    smoothed = jnp.dot(power, smoother(F, FB, HALF), precision=lax.Precision.HIGHEST)
    divisor = jnp.sqrt(smoothed + eps_power)
    whitened = jnp.stack([real_part[:, :FB] / divisor, imag_part[:, :FB] / divisor], axis=1)
    whitened = whitened.reshape(window_count, channel_count, 2, FB)
    return jnp.transpose(whitened, (1, 0, 2, 3)).astype(jnp.bfloat16)

def whiten(records, starts):
    windows = jax.vmap(lambda window_start: lax.dynamic_slice_in_dim(records, window_start, RAW, 1))(starts)
    traces = decimate(windows)
    spectrum = jnp.fft.rfft(traces, axis=-1)[:, :, :F]
    real_part = jnp.real(spectrum).reshape(-1, F)
    imag_part = jnp.imag(spectrum).reshape(-1, F)
    return finish(real_part, imag_part, traces.shape[0], traces.shape[1])

def lag_table(band, lag_count, samples):
    bin_ids = jnp.arange(band, dtype=jnp.int32)[:, None]
    lag_ids = jnp.arange(lag_count, dtype=jnp.int32)[None, :] - lag_count // 2 + samples
    phase_index = bin_ids * lag_ids % samples
    radians = 2.0 * math.pi / samples * phase_index.astype(jnp.float32)
    return jnp.concatenate([jnp.cos(radians), -jnp.sin(radians)], axis=0).astype(jnp.bfloat16)

def correlate(sources, receivers, inverse):
    sources = sources.astype(jnp.float32)
    receivers = receivers.astype(jnp.float32)

    def pair_sum(first_side, second_side):
        return jnp.einsum('iwf,jwf->ijf', first_side, second_side)
    cross_real = pair_sum(sources[:, :, 0], receivers[:, :, 0]) + pair_sum(sources[:, :, 1], receivers[:, :, 1])
    cross_imag = pair_sum(sources[:, :, 1], receivers[:, :, 0]) - pair_sum(sources[:, :, 0], receivers[:, :, 1])
    cross = jnp.concatenate([cross_real, cross_imag], axis=2).astype(jnp.bfloat16)
    cross = cross.reshape(-1, cross.shape[2])
    return jnp.dot(cross, inverse, preferred_element_type=jnp.float32)

def reference(records, starts, block_mask):
    spectra = whiten(records, starts)
    inverse = lag_table(FB, LAGS, NT)
    normalizer = 1.0 / math.sqrt(WINDOWS * FB)
    blocks = spectra.reshape(BLOCKS, BLOCK, WINDOWS, 2, FB)
    local_ids = jnp.arange(BLOCK, dtype=jnp.int32)

    def one_pair(src_block, rcv_block):
        lagged = correlate(blocks[src_block], blocks[rcv_block], inverse).reshape(BLOCK, BLOCK, LAGS) * normalizer
        source_ids = src_block * BLOCK + local_ids
        receiver_ids = rcv_block * BLOCK + local_ids
        allowed = jnp.repeat(block_mask[src_block, rcv_block], CH_DEV)
        keep_pair = (source_ids[:, None] < receiver_ids[None, :]) & (allowed[None, :] > 0)
        return jnp.where(keep_pair[:, :, None], lagged, 0.0).astype(jnp.bfloat16)

    def row_of(src_block):

        def column_of(rcv_block):
            return lax.cond(rcv_block >= src_block, lambda: one_pair(src_block, rcv_block), lambda: jnp.zeros((BLOCK, BLOCK, LAGS), jnp.bfloat16))
        columns = lax.map(column_of, jnp.arange(BLOCKS, dtype=jnp.int32))
        return jnp.transpose(columns, (1, 0, 2, 3))
    rows_all = lax.map(row_of, jnp.arange(BLOCKS, dtype=jnp.int32))
    return rows_all.reshape(CHANNELS, BLOCKS, SUBS, CH_DEV, LAGS)
```

```python
import functools
import math

import jax
import jax.numpy as jnp
import ml_dtypes
import numpy as np
from jax import lax
from jax.experimental import pallas as pl
from jax.experimental.pallas import tpu as pltpu
from jax.sharding import PartitionSpec as P

DEC = 5
NT = 2048
FB = 512
HALF = 64
LAGS = 128
TAPS = 65
F = 1024
LANES = 128
WINDOWS = 2
CH = 8

CHUNKS = NT // LANES
STRIDE = DEC * LANES
SPAN = 7 * LANES
RESID = 200
SUB_BINS = FB // CHUNKS
MORE_BINS = HALF // CHUNKS
GROUPS = CHUNKS // 2

eps_power = 1e-06
MESH = pl.DeviceIdType.MESH


def residues(group):
    return (0, CHUNKS // 2) if group == 0 else (group, CHUNKS - group)


def halves(table):
    high = table.astype(ml_dtypes.bfloat16)
    low = (table - high.astype(np.float64)).astype(ml_dtypes.bfloat16)
    return np.stack([high, low])


def band_matrix():
    tap = np.arange(TAPS, dtype=np.float64)
    taper = 0.5 - 0.5 * np.cos(2.0 * math.pi * (tap + 1.0) / (TAPS + 1.0))
    taps = np.sinc((tap - (TAPS - 1) / 2.0) / DEC) * taper / DEC
    k = np.arange(SPAN + RESID)[:, None] - RESID - DEC * np.arange(LANES)[None, :]
    return np.where((k >= 0) & (k < TAPS), taps[np.clip(k, 0, TAPS - 1)], 0.0).astype(np.float32)


def transform_tables():
    n0 = np.arange(LANES)[:, None]
    tables = np.zeros((GROUPS, 2 * LANES, 2 * LANES))
    band = np.zeros(FB, np.int64)
    beyond = np.zeros(LANES, np.int64)
    for g in range(GROUPS):
        re_at, im_at = (0, LANES // 2) if g % 2 == 0 else (LANES // 2, 0)
        for which, f0 in enumerate(residues(g)):
            for f1 in range(SUB_BINS + MORE_BINS):
                f = CHUNKS * f1 + f0
                if f1 < SUB_BINS:
                    col_re = re_at + which * SUB_BINS + f1
                    col_im = im_at + which * SUB_BINS + f1
                    band[g * 2 * SUB_BINS + which * SUB_BINS + f1] = f
                else:
                    lane = g * 2 * MORE_BINS + which * MORE_BINS + f1 - SUB_BINS
                    col_re = LANES + lane
                    col_im = LANES + LANES // 2 + lane
                    beyond[lane] = beyond[LANES // 2 + lane] = f
                phase = 2.0 * math.pi / NT * (n0[:, 0] * f % NT)
                cos, sin = np.cos(phase), np.sin(phase)
                if g == 0:
                    rows = slice(which * LANES, (which + 1) * LANES)
                    tables[g, rows, col_re] = cos
                    tables[g, rows, col_im] = -sin
                else:
                    sign = 1.0 if which == 0 else -1.0
                    tables[g, :LANES, col_re] = cos
                    tables[g, LANES:, col_re] = sign * sin
                    tables[g, :LANES, col_im] = -sin
                    tables[g, LANES:, col_im] = sign * cos
    return tables, band, beyond


def constants():
    tables, band, beyond = transform_tables()
    source = np.concatenate([band, beyond])[:, None]
    inside = (np.abs(source - band[None, :]) <= HALF).astype(ml_dtypes.bfloat16)
    count = np.minimum(band + HALF, F - 1) - np.maximum(band - HALF, 0) + 1
    per_bin = (1.0 / count).astype(np.float32)[None, :]
    phase = 2.0 * math.pi / NT * (band[:, None] * (np.arange(LAGS)[None, :] - LAGS // 2 + NT) % NT)
    lags = np.concatenate([np.cos(phase), -np.sin(phase)]).astype(np.float32)
    lags = lags.astype(ml_dtypes.bfloat16).astype(np.float32) / math.sqrt(WINDOWS * FB)
    return band_matrix(), halves(tables), inside, per_bin, lags.astype(ml_dtypes.bfloat16)


def real_dft(x):
    n = len(x)
    if n == 2:
        return [(x[0] + x[1], None), (x[0] - x[1], None)]
    half = n // 2
    even = real_dft([x[b] + x[b + half] for b in range(half)])
    odd = [x[b] - x[b + half] for b in range(half)]
    out = [None] * (half + 1)
    out[::2] = even
    for f in range(1, half, 2):
        re = odd[0]
        im = odd[half // 2] * -math.sin(math.pi * f / 2)
        for b in range(1, half // 2):
            re = re + (odd[b] - odd[half - b]) * math.cos(2 * math.pi * f * b / n)
            im = im - (odd[b] + odd[half - b]) * math.sin(2 * math.pi * f * b / n)
        out[f] = (re, im)
    return out


def split(x):
    high = x.astype(jnp.bfloat16)
    return high, (x - high.astype(jnp.float32)).astype(jnp.bfloat16)


def dot(a, b):
    return jnp.dot(a, b, preferred_element_type=jnp.float32)


def both_halves(x, table_high, table_low):
    rows = x.shape[0]
    high, low = split(x)
    top = dot(jnp.concatenate([high, low], axis=0), table_high)
    return top[:rows] + top[rows:] + dot(high, table_low)


def flip(index, mask, bits):
    for b in range(bits):
        bit = 1 << b
        index = index + (mask // bit % 2) * bit * (1 - 2 * (index // bit % 2))
    return index


def whiten(starts, records, band, tables, inside, per_bin, waits):
    traces = []
    for w in range(WINDOWS):
        start = starts[w]
        last = records.shape[1] - STRIDE * (CHUNKS - 1) - SPAN
        base = jnp.minimum(start // LANES * LANES, last)
        if w == 0:
            waits[0]()
        raw = jnp.concatenate(
            [
                records[:, pl.ds(pl.multiple_of(base + STRIDE * b, LANES), SPAN)]
                for b in range(CHUNKS)
            ],
            axis=0,
        )
        taps_high, taps_low = split(band[pl.ds(RESID - (start - base), SPAN), :])
        traces.append(both_halves(raw, taps_high, taps_low))
    pieces = [
        jnp.concatenate([t[CH * b : CH * (b + 1)] for t in traces], axis=0) for b in range(CHUNKS)
    ]
    bins = real_dft(pieces)
    waits[1]()
    outs = []
    for g in range(GROUPS):
        if g == 0:
            x = jnp.concatenate([bins[0][0], bins[CHUNKS // 2][0]], axis=1)
        else:
            x = jnp.concatenate(bins[g], axis=1)
        outs.append(both_halves(x, tables[0, g], tables[1, g]))
    beyond = functools.reduce(lambda a, b: a + b, [o[:, LANES:] for o in outs])
    first = lax.broadcasted_iota(jnp.int32, (WINDOWS * CH, LANES), 1) < LANES // 2
    re, im = [], []
    for q in range(GROUPS // 2):
        a, b = outs[2 * q][:, :LANES], outs[2 * q + 1][:, :LANES]
        re.append(jnp.where(first, a, b))
        im.append(pltpu.roll(jnp.where(first, b, a), LANES // 2, 1))
    re, im = jnp.concatenate(re, axis=1), jnp.concatenate(im, axis=1)
    power = jnp.concatenate([re * re + im * im, beyond * beyond], axis=1)
    waits[2]()
    both = dot(jnp.concatenate(split(power), axis=0), inside[...])
    smoothed = (both[: WINDOWS * CH] + both[WINDOWS * CH :]) * per_bin[...]
    scale = lax.rsqrt(smoothed + eps_power)
    return jnp.concatenate([re * scale, im * scale], axis=1).astype(jnp.bfloat16)


def spectra_kernel(
    starts, per_bin, records_hbm, band_hbm, tables_hbm, inside_hbm, out,
    records, band, tables, inside, load_sem,
):
    loads = [
        pltpu.make_async_copy(a, b, load_sem.at[i])
        for i, (a, b) in enumerate(
            [(records_hbm, records), (band_hbm, band), (tables_hbm, tables), (inside_hbm, inside)]
        )
    ]
    for load in loads:
        load.start()

    def first_wait():
        loads[0].wait()
        loads[1].wait()

    out[...] = whiten(
        starts, records, band, tables, inside, per_bin, [first_wait, loads[2].wait, loads[3].wait]
    )


def pair_kernel(
    n_src, n_rcv, mask, own, lags_hbm, out,
    lags, src_buf, rcv_buf, src_f32, rcv_f32, cross, threshold,
    load_sem, src_send, src_recv, rcv_send, rcv_recv,
):
    me_s, me_r = lax.axis_index("src"), lax.axis_index("rcv")
    src_bits, rcv_bits = n_src.bit_length() - 1, n_rcv.bit_length() - 1
    load = pltpu.make_async_copy(lags_hbm, lags, load_sem)
    load.start()

    barrier = pltpu.get_barrier_semaphore()

    def greet_src(k, _):
        peer = flip(me_s, k, src_bits)
        pl.semaphore_signal(barrier, inc=1, device_id={"src": peer}, device_id_type=MESH)
        return 0

    def greet_rcv(k, _):
        peer = flip(me_r, k, rcv_bits)
        pl.semaphore_signal(barrier, inc=1, device_id={"rcv": peer}, device_id_type=MESH)
        return 0

    lax.fori_loop(1, n_src, greet_src, 0)
    lax.fori_loop(1, n_rcv, greet_rcv, 0)

    src_buf[me_s] = own[...]
    rcv_buf[me_r] = own[...]
    pl.semaphore_wait(barrier, n_src + n_rcv - 2)

    def src_copy(slot, peer):
        return pltpu.make_async_remote_copy(
            src_ref=src_buf.at[slot], dst_ref=src_buf.at[slot], send_sem=src_send.at[peer],
            recv_sem=src_recv.at[slot], device_id={"src": peer}, device_id_type=MESH,
        )

    def rcv_copy(slot, peer):
        return pltpu.make_async_remote_copy(
            src_ref=rcv_buf.at[slot], dst_ref=rcv_buf.at[slot], send_sem=rcv_send.at[peer],
            recv_sem=rcv_recv.at[slot], device_id={"rcv": peer}, device_id_type=MESH,
        )

    def send_rcv(k, _):
        rcv_copy(me_r, flip(me_r, k, rcv_bits)).start()
        return 0

    def send_src(k, _):
        src_copy(me_s, flip(me_s, k, src_bits)).start()
        return 0

    lax.fori_loop(1, n_rcv, send_rcv, 0)
    lax.fori_loop(1, n_src, send_src, 0)

    block_rows = n_src * CH
    for b in range(n_rcv):
        ids = lax.broadcasted_iota(jnp.int32, (CH, LAGS), 0) + b * block_rows + me_s * CH
        threshold[CH * b : CH * (b + 1), :] = jnp.where(mask[0, b, 0] > 0, ids, -1)

    def land_rcv(k, _):
        peer = flip(me_r, k, rcv_bits)

        @pl.when(k > 0)
        def _():
            rcv_copy(peer, peer).wait_recv()

        held = rcv_buf[peer].astype(jnp.float32)
        for w in range(WINDOWS):
            rcv_f32[w, pl.ds(pl.multiple_of(peer * CH, CH), CH), :] = held[w * CH : (w + 1) * CH]
        return 0

    lax.fori_loop(0, n_rcv, land_rcv, 0)
    load.wait()

    rows = n_rcv * CH
    part = min(rows, 32)

    def per_source(k, _):
        peer = flip(me_s, k, src_bits)

        @pl.when(k > 0)
        def _():
            src_copy(peer, peer).wait_recv()

        src_f32[...] = src_buf[peer].astype(jnp.float32)
        for at in range(0, rows, part):
            for q in range(FB // LANES):
                lo, hi = q * LANES, FB + q * LANES
                held = [
                    (rcv_f32[w, at : at + part, lo : lo + LANES], rcv_f32[w, at : at + part, hi : hi + LANES])
                    for w in range(WINDOWS)
                ]
                for c in range(CH):
                    re = im = None
                    for w in range(WINDOWS):
                        row = w * CH + c
                        s_re = src_f32[row : row + 1, lo : lo + LANES]
                        s_im = src_f32[row : row + 1, hi : hi + LANES]
                        r_re, r_im = held[w]
                        one = s_re * r_re + s_im * r_im
                        two = s_im * r_re - s_re * r_im
                        re = one if re is None else re + one
                        im = two if im is None else im + two
                    to = c * rows + at
                    cross[to : to + part, lo : lo + LANES] = re.astype(jnp.bfloat16)
                    cross[to : to + part, hi : hi + LANES] = im.astype(jnp.bfloat16)
        lagged = dot(cross[...], lags[...])
        first_id = me_r * block_rows + peer * CH
        for c in range(CH):
            keep = threshold[...] > first_id + c
            value = jnp.where(keep, lagged[c * rows : (c + 1) * rows], 0.0)
            out[peer * CH + c] = value.astype(jnp.bfloat16)
        return 0

    lax.fori_loop(0, n_src, per_source, 0)

    def sent_src(k, _):
        src_copy(me_s, flip(me_s, k, src_bits)).wait_send()
        return 0

    def sent_rcv(k, _):
        rcv_copy(me_r, flip(me_r, k, rcv_bits)).wait_send()
        return 0

    lax.fori_loop(1, n_src, sent_src, 0)
    lax.fori_loop(1, n_rcv, sent_rcv, 0)


def on_device(n_src, n_rcv, records, starts, block_mask):
    band, tables, inside, per_bin, lags = constants()
    rows = n_rcv * CH
    held = (WINDOWS * CH, 2 * FB)
    smem = pl.BlockSpec(memory_space=pltpu.SMEM)
    vmem = pl.BlockSpec(memory_space=pltpu.VMEM)
    anywhere = pl.BlockSpec(memory_space=pl.ANY)
    own = pl.pallas_call(
        spectra_kernel,
        out_shape=jax.ShapeDtypeStruct(held, jnp.bfloat16),
        in_specs=[smem, vmem] + [anywhere] * 4,
        out_specs=vmem,
        scratch_shapes=[
            pltpu.VMEM(records.shape, jnp.float32),
            pltpu.VMEM(band.shape, jnp.float32),
            pltpu.VMEM(tables.shape, jnp.bfloat16),
            pltpu.VMEM(inside.shape, jnp.bfloat16),
            pltpu.SemaphoreType.DMA((4,)),
        ],
        compiler_params=pltpu.CompilerParams(vmem_limit_bytes=32 * 1024 * 1024),
    )(starts, per_bin, records, band, tables, inside)
    result = pl.pallas_call(
        functools.partial(pair_kernel, n_src, n_rcv),
        out_shape=jax.ShapeDtypeStruct((n_src * CH, rows, LAGS), jnp.bfloat16),
        in_specs=[smem, vmem, anywhere],
        out_specs=vmem,
        scratch_shapes=[
            pltpu.VMEM(lags.shape, jnp.bfloat16),
            pltpu.VMEM((n_src,) + held, jnp.bfloat16),
            pltpu.VMEM((n_rcv,) + held, jnp.bfloat16),
            pltpu.VMEM(held, jnp.float32),
            pltpu.VMEM((WINDOWS, rows, 2 * FB), jnp.float32),
            pltpu.VMEM((CH * rows, 2 * FB), jnp.bfloat16),
            pltpu.VMEM((rows, LAGS), jnp.int32),
            pltpu.SemaphoreType.DMA,
            pltpu.SemaphoreType.DMA((n_src,)),
            pltpu.SemaphoreType.DMA((n_src,)),
            pltpu.SemaphoreType.DMA((n_rcv,)),
            pltpu.SemaphoreType.DMA((n_rcv,)),
        ],
        compiler_params=pltpu.CompilerParams(
            collective_id=0, has_side_effects=True, vmem_limit_bytes=32 * 1024 * 1024
        ),
    )(block_mask, own, lags)
    return result.reshape(n_src * CH, n_rcv, 1, CH, LAGS)


def solution(mesh):
    in_specs = (P(("rcv", "src"), None), P(), P("rcv", None, "src"))
    out_specs = P("rcv", None, "src", None, None)
    return jax.shard_map(
        functools.partial(on_device, mesh.shape["src"], mesh.shape["rcv"]),
        mesh=mesh, in_specs=in_specs, out_specs=out_specs, check_vma=False,
    )
```

```python
import functools
import math

import jax
import jax.numpy as jnp
import ml_dtypes
import numpy as np
from jax import lax
from jax.experimental import pallas as pl
from jax.experimental.pallas import tpu as pltpu
from jax.sharding import PartitionSpec as P

DEC = 5
NT = 2048
FB = 512
HALF = 64
LAGS = 128
TAPS = 65
F = 1024
LANES = 128
WINDOWS = 2
CH = 8

CHUNKS = NT // LANES
STRIDE = DEC * LANES
SPAN = 7 * LANES
RESID = 200
SUB_BINS = FB // CHUNKS
MORE_BINS = HALF // CHUNKS
GROUPS = CHUNKS // 2

eps_power = 1e-06
MESH = pl.DeviceIdType.MESH


def residues(group):
    return (0, CHUNKS // 2) if group == 0 else (group, CHUNKS - group)


def halves(table):
    high = table.astype(ml_dtypes.bfloat16)
    low = (table - high.astype(np.float64)).astype(ml_dtypes.bfloat16)
    return np.stack([high, low])


def band_matrix():
    tap = np.arange(TAPS, dtype=np.float64)
    taper = 0.5 - 0.5 * np.cos(2.0 * math.pi * (tap + 1.0) / (TAPS + 1.0))
    taps = np.sinc((tap - (TAPS - 1) / 2.0) / DEC) * taper / DEC
    k = np.arange(SPAN + RESID)[:, None] - RESID - DEC * np.arange(LANES)[None, :]
    return np.where((k >= 0) & (k < TAPS), taps[np.clip(k, 0, TAPS - 1)], 0.0).astype(np.float32)


def transform_tables():
    n0 = np.arange(LANES)[:, None]
    tables = np.zeros((GROUPS, 2 * LANES, 2 * LANES))
    band = np.zeros(FB, np.int64)
    beyond = np.zeros(LANES, np.int64)
    for g in range(GROUPS):
        re_at, im_at = (0, LANES // 2) if g % 2 == 0 else (LANES // 2, 0)
        for which, f0 in enumerate(residues(g)):
            for f1 in range(SUB_BINS + MORE_BINS):
                f = CHUNKS * f1 + f0
                if f1 < SUB_BINS:
                    col_re = re_at + which * SUB_BINS + f1
                    col_im = im_at + which * SUB_BINS + f1
                    band[g * 2 * SUB_BINS + which * SUB_BINS + f1] = f
                else:
                    lane = g * 2 * MORE_BINS + which * MORE_BINS + f1 - SUB_BINS
                    col_re = LANES + lane
                    col_im = LANES + LANES // 2 + lane
                    beyond[lane] = beyond[LANES // 2 + lane] = f
                phase = 2.0 * math.pi / NT * (n0[:, 0] * f % NT)
                cos, sin = np.cos(phase), np.sin(phase)
                if g == 0:
                    rows = slice(which * LANES, (which + 1) * LANES)
                    tables[g, rows, col_re] = cos
                    tables[g, rows, col_im] = -sin
                else:
                    sign = 1.0 if which == 0 else -1.0
                    tables[g, :LANES, col_re] = cos
                    tables[g, LANES:, col_re] = sign * sin
                    tables[g, :LANES, col_im] = -sin
                    tables[g, LANES:, col_im] = sign * cos
    return tables, band, beyond


def constants():
    tables, band, beyond = transform_tables()
    source = np.concatenate([band, beyond])[:, None]
    inside = (np.abs(source - band[None, :]) <= HALF).astype(ml_dtypes.bfloat16)
    count = np.minimum(band + HALF, F - 1) - np.maximum(band - HALF, 0) + 1
    per_bin = (1.0 / count).astype(np.float32)[None, :]
    phase = 2.0 * math.pi / NT * (band[:, None] * (np.arange(LAGS)[None, :] - LAGS // 2 + NT) % NT)
    lags = np.concatenate([np.cos(phase), -np.sin(phase)]).astype(np.float32)
    lags = lags.astype(ml_dtypes.bfloat16).astype(np.float32) / math.sqrt(WINDOWS * FB)
    return band_matrix(), halves(tables), inside, per_bin, lags.astype(ml_dtypes.bfloat16)


def real_dft(x):
    n = len(x)
    if n == 2:
        return [(x[0] + x[1], None), (x[0] - x[1], None)]
    half = n // 2
    even = real_dft([x[b] + x[b + half] for b in range(half)])
    odd = [x[b] - x[b + half] for b in range(half)]
    out = [None] * (half + 1)
    out[::2] = even
    for f in range(1, half, 2):
        re = odd[0]
        im = odd[half // 2] * -math.sin(math.pi * f / 2)
        for b in range(1, half // 2):
            re = re + (odd[b] - odd[half - b]) * math.cos(2 * math.pi * f * b / n)
            im = im - (odd[b] + odd[half - b]) * math.sin(2 * math.pi * f * b / n)
        out[f] = (re, im)
    return out


def split(x):
    high = x.astype(jnp.bfloat16)
    return high, (x - high.astype(jnp.float32)).astype(jnp.bfloat16)


def dot(a, b):
    return jnp.dot(a, b, preferred_element_type=jnp.float32)


def both_halves(x, table_high, table_low):
    rows = x.shape[0]
    high, low = split(x)
    top = dot(jnp.concatenate([high, low], axis=0), table_high)
    return top[:rows] + top[rows:] + dot(high, table_low)


def flip(index, mask, bits):
    for b in range(bits):
        bit = 1 << b
        index = index + (mask // bit % 2) * bit * (1 - 2 * (index // bit % 2))
    return index


def whiten(starts, records, band, tables, inside, per_bin, waits):
    traces = []
    for w in range(WINDOWS):
        start = starts[w]
        last = records.shape[1] - STRIDE * (CHUNKS - 1) - SPAN
        base = jnp.minimum(start // LANES * LANES, last)
        if w == 0:
            waits[0]()
        raw = jnp.concatenate(
            [
                records[:, pl.ds(pl.multiple_of(base + STRIDE * b, LANES), SPAN)]
                for b in range(CHUNKS)
            ],
            axis=0,
        )
        taps_high, taps_low = split(band[pl.ds(RESID - (start - base), SPAN), :])
        traces.append(both_halves(raw, taps_high, taps_low))
    pieces = [
        jnp.concatenate([t[CH * b : CH * (b + 1)] for t in traces], axis=0) for b in range(CHUNKS)
    ]
    bins = real_dft(pieces)
    waits[1]()
    outs = []
    for g in range(GROUPS):
        if g == 0:
            x = jnp.concatenate([bins[0][0], bins[CHUNKS // 2][0]], axis=1)
        else:
            x = jnp.concatenate(bins[g], axis=1)
        outs.append(both_halves(x, tables[0, g], tables[1, g]))
    beyond = functools.reduce(lambda a, b: a + b, [o[:, LANES:] for o in outs])
    first = lax.broadcasted_iota(jnp.int32, (WINDOWS * CH, LANES), 1) < LANES // 2
    re, im = [], []
    for q in range(GROUPS // 2):
        a, b = outs[2 * q][:, :LANES], outs[2 * q + 1][:, :LANES]
        re.append(jnp.where(first, a, b))
        im.append(pltpu.roll(jnp.where(first, b, a), LANES // 2, 1))
    re, im = jnp.concatenate(re, axis=1), jnp.concatenate(im, axis=1)
    power = jnp.concatenate([re * re + im * im, beyond * beyond], axis=1)
    waits[2]()
    both = dot(jnp.concatenate(split(power), axis=0), inside[...])
    smoothed = (both[: WINDOWS * CH] + both[WINDOWS * CH :]) * per_bin[...]
    scale = lax.rsqrt(smoothed + eps_power)
    return jnp.concatenate([re * scale, im * scale], axis=1).astype(jnp.bfloat16)


def spectra_kernel(
    starts, records_hbm, band_hbm, tables_hbm, inside_hbm, per_bin_hbm, out,
    records, band, tables, inside, per_bin, load_sem,
):
    loads = [
        pltpu.make_async_copy(a, b, load_sem.at[i])
        for i, (a, b) in enumerate(
            [(records_hbm, records), (band_hbm, band), (tables_hbm, tables), (inside_hbm, inside),
             (per_bin_hbm, per_bin)]
        )
    ]
    for load in loads:
        load.start()

    def first_wait():
        loads[0].wait()
        loads[1].wait()

    def last_wait():
        loads[3].wait()
        loads[4].wait()

    out[...] = whiten(
        starts, records, band, tables, inside, per_bin, [first_wait, loads[2].wait, last_wait]
    )


def pair_kernel(
    n_src, n_rcv, mask, own, lags_hbm, out,
    lags, src_buf, rcv_buf, src_f32, rcv_buf2, cross_even, cross_odd, threshold,
    load_sem, src_send, src_recv, rcv_send, rcv_recv,
):
    me_s, me_r = lax.axis_index("src"), lax.axis_index("rcv")
    src_bits, rcv_bits = n_src.bit_length() - 1, n_rcv.bit_length() - 1
    load = pltpu.make_async_copy(lags_hbm, lags, load_sem)
    load.start()

    barrier = pltpu.get_barrier_semaphore()

    def greet_src(k, _):
        peer = flip(me_s, k, src_bits)
        pl.semaphore_signal(barrier, inc=1, device_id={"src": peer}, device_id_type=MESH)
        return 0

    def greet_rcv(k, _):
        peer = flip(me_r, k, rcv_bits)
        pl.semaphore_signal(barrier, inc=1, device_id={"rcv": peer}, device_id_type=MESH)
        return 0

    lax.fori_loop(1, n_src, greet_src, 0)
    lax.fori_loop(1, n_rcv, greet_rcv, 0)

    src_buf[me_s] = own[...]
    rcv_buf[me_r] = own[...]
    pl.semaphore_wait(barrier, n_src + n_rcv - 2)

    def src_copy(slot, peer):
        return pltpu.make_async_remote_copy(
            src_ref=src_buf.at[slot], dst_ref=src_buf.at[slot], send_sem=src_send.at[peer],
            recv_sem=src_recv.at[slot], device_id={"src": peer}, device_id_type=MESH,
        )

    def rcv_copy(slot, peer):
        return pltpu.make_async_remote_copy(
            src_ref=rcv_buf.at[slot], dst_ref=rcv_buf.at[slot], send_sem=rcv_send.at[peer],
            recv_sem=rcv_recv.at[slot], device_id={"rcv": peer}, device_id_type=MESH,
        )

    def send_rcv(k, _):
        peer = flip(me_r, k, rcv_bits)

        @pl.when(peer < me_r)
        def _():
            rcv_copy(me_r, peer).start()

        return 0

    def send_src(k, _):
        src_copy(me_s, flip(me_s, k, src_bits)).start()
        return 0

    lax.fori_loop(1, n_rcv, send_rcv, 0)
    lax.fori_loop(1, n_src, send_src, 0)

    block_rows = n_src * CH
    for b in range(n_rcv):
        ids = lax.broadcasted_iota(jnp.int32, (CH, LAGS), 0) + b * block_rows + me_s * CH
        threshold[CH * b : CH * (b + 1), :] = jnp.where(mask[0, b] > 0, ids, -1)

    def clear_rcv(k, _):
        rcv_buf[k] = jnp.zeros(rcv_buf.shape[1:], rcv_buf.dtype)
        return 0

    def land_rcv(k, _):
        rcv_copy(k, k).wait_recv()
        return 0

    lax.fori_loop(0, me_r, clear_rcv, 0)
    lax.fori_loop(me_r + 1, n_rcv, land_rcv, 0)
    for b in range(0, n_rcv, 2):
        for w in range(WINDOWS):
            at = slice(w * CH, (w + 1) * CH)
            pair = [rcv_buf[b + i].astype(jnp.float32)[at] for i in range(2)]
            rcv_buf2[w, b * CH : (b + 2) * CH, :] = jnp.concatenate(pair, axis=0).astype(jnp.bfloat16)
    load.wait()

    rows = n_rcv * CH
    part = min(rows, 32)

    def products(k, cross):
        peer = flip(me_s, k, src_bits)
        src_f32[...] = src_buf[peer].astype(jnp.float32)
        for at in range(0, rows, part):
            for q in range(FB // LANES):
                lo, hi = q * LANES, FB + q * LANES
                held = [
                    (rcv_buf2[w, at : at + part, lo : lo + LANES], rcv_buf2[w, at : at + part, hi : hi + LANES])
                    for w in range(WINDOWS)
                ]
                for c in range(CH):
                    re = im = None
                    for w in range(WINDOWS):
                        row = w * CH + c
                        s_re, s_im = [
                            jnp.broadcast_to(src_f32[row : row + 1, x : x + LANES], (part, LANES)).astype(jnp.bfloat16)
                            for x in (lo, hi)
                        ]
                        r_re, r_im = held[w]
                        one = s_re * r_re + s_im * r_im
                        two = s_im * r_re - s_re * r_im
                        re = one if re is None else re + one
                        im = two if im is None else im + two
                    to = c * rows + at
                    cross[to : to + part, lo : lo + LANES] = re
                    cross[to : to + part, hi : hi + LANES] = im

    def lagged(k, cross):
        peer = flip(me_s, k, src_bits)
        values = dot(cross[...], lags[...])
        first_id = me_r * block_rows + peer * CH
        for c in range(CH):
            keep = threshold[...] > first_id + c
            value = jnp.where(keep, values[c * rows : (c + 1) * rows], 0.0)
            out[peer * CH + c] = value.astype(jnp.bfloat16)

    def arrive(k):
        peer = flip(me_s, k, src_bits)
        src_copy(peer, peer).wait_recv()

    products(0, cross_even)

    def two_sources(t, _):
        arrive(2 * t + 1)
        products(2 * t + 1, cross_odd)
        lagged(2 * t, cross_even)
        arrive(2 * t + 2)
        products(2 * t + 2, cross_even)
        lagged(2 * t + 1, cross_odd)
        return 0

    lax.fori_loop(0, n_src // 2 - 1, two_sources, 0)
    arrive(n_src - 1)
    products(n_src - 1, cross_odd)
    lagged(n_src - 2, cross_even)
    lagged(n_src - 1, cross_odd)

    def sent_src(k, _):
        src_copy(me_s, flip(me_s, k, src_bits)).wait_send()
        return 0

    def sent_rcv(k, _):
        rcv_copy(me_r, k).wait_send()
        return 0

    lax.fori_loop(1, n_src, sent_src, 0)
    lax.fori_loop(0, me_r, sent_rcv, 0)


def on_device(n_src, n_rcv, records, starts, block_mask):
    band, tables, inside, per_bin, lags = constants()
    rows = n_rcv * CH
    held = (WINDOWS * CH, 2 * FB)
    smem = pl.BlockSpec(memory_space=pltpu.SMEM)
    vmem = pl.BlockSpec(memory_space=pltpu.VMEM)
    anywhere = pl.BlockSpec(memory_space=pl.ANY)
    own = pl.pallas_call(
        spectra_kernel,
        out_shape=jax.ShapeDtypeStruct(held, jnp.bfloat16),
        in_specs=[smem] + [anywhere] * 5,
        out_specs=vmem,
        scratch_shapes=[
            pltpu.VMEM(records.shape, jnp.float32),
            pltpu.VMEM(band.shape, jnp.float32),
            pltpu.VMEM(tables.shape, jnp.bfloat16),
            pltpu.VMEM(inside.shape, jnp.bfloat16),
            pltpu.VMEM(per_bin.shape, jnp.float32),
            pltpu.SemaphoreType.DMA((5,)),
        ],
        compiler_params=pltpu.CompilerParams(vmem_limit_bytes=60 * 1024 * 1024),
    )(starts, records, band, tables, inside, per_bin)
    result = pl.pallas_call(
        functools.partial(pair_kernel, n_src, n_rcv),
        out_shape=jax.ShapeDtypeStruct((n_src * CH, rows, LAGS), jnp.bfloat16),
        in_specs=[smem, vmem, anywhere],
        out_specs=vmem,
        scratch_shapes=[
            pltpu.VMEM(lags.shape, jnp.bfloat16),
            pltpu.VMEM((n_src,) + held, jnp.bfloat16),
            pltpu.VMEM((n_rcv,) + held, jnp.bfloat16),
            pltpu.VMEM(held, jnp.float32),
            pltpu.VMEM((WINDOWS, rows, 2 * FB), jnp.bfloat16),
            pltpu.VMEM((CH * rows, 2 * FB), jnp.bfloat16),
            pltpu.VMEM((CH * rows, 2 * FB), jnp.bfloat16),
            pltpu.VMEM((rows, LAGS), jnp.int32),
            pltpu.SemaphoreType.DMA,
            pltpu.SemaphoreType.DMA((n_src,)),
            pltpu.SemaphoreType.DMA((n_src,)),
            pltpu.SemaphoreType.DMA((n_rcv,)),
            pltpu.SemaphoreType.DMA((n_rcv,)),
        ],
        compiler_params=pltpu.CompilerParams(
            collective_id=0, has_side_effects=True, vmem_limit_bytes=60 * 1024 * 1024
        ),
    )(block_mask.reshape(1, n_rcv), own, lags)
    return result.reshape(n_src * CH, n_rcv, 1, CH, LAGS)


def solution(mesh):
    in_specs = (P(("rcv", "src"), None), P(), P("rcv", None, "src"))
    out_specs = P("rcv", None, "src", None, None)
    return jax.shard_map(
        functools.partial(on_device, mesh.shape["src"], mesh.shape["rcv"]),
        mesh=mesh, in_specs=in_specs, out_specs=out_specs, check_vma=False,
    )
```

```python
import functools
import math

import jax
import jax.numpy as jnp
import ml_dtypes
import numpy as np
from jax import lax
from jax.experimental import pallas as pl
from jax.experimental.pallas import tpu as pltpu
from jax.sharding import PartitionSpec as P

DEC = 5
NT = 2048
FB = 512
HALF = 64
LAGS = 128
TAPS = 65
F = 1024
LANES = 128
WINDOWS = 2
CH = 8
PAIR = 2 * CH

CHUNKS = NT // LANES
STRIDE = DEC * LANES
SPAN = 7 * LANES
RESID = 200
SUB_BINS = FB // CHUNKS
MORE_BINS = HALF // CHUNKS
GROUPS = CHUNKS // 2

eps_power = 1e-06
MESH = pl.DeviceIdType.MESH


def residues(group):
    return (0, CHUNKS // 2) if group == 0 else (group, CHUNKS - group)


def halves(table):
    high = table.astype(ml_dtypes.bfloat16)
    low = (table - high.astype(np.float64)).astype(ml_dtypes.bfloat16)
    return np.stack([high, low])


def band_matrix():
    tap = np.arange(TAPS, dtype=np.float64)
    taper = 0.5 - 0.5 * np.cos(2.0 * math.pi * (tap + 1.0) / (TAPS + 1.0))
    taps = np.sinc((tap - (TAPS - 1) / 2.0) / DEC) * taper / DEC
    k = np.arange(SPAN + RESID)[:, None] - RESID - DEC * np.arange(LANES)[None, :]
    return np.where((k >= 0) & (k < TAPS), taps[np.clip(k, 0, TAPS - 1)], 0.0).astype(np.float32)


def transform_tables():
    n0 = np.arange(LANES)[:, None]
    tables = np.zeros((GROUPS, 2 * LANES, 2 * LANES))
    band = np.zeros(FB, np.int64)
    beyond = np.zeros(LANES, np.int64)
    for g in range(GROUPS):
        re_at, im_at = (0, LANES // 2) if g % 2 == 0 else (LANES // 2, 0)
        for which, f0 in enumerate(residues(g)):
            for f1 in range(SUB_BINS + MORE_BINS):
                f = CHUNKS * f1 + f0
                if f1 < SUB_BINS:
                    col_re = re_at + which * SUB_BINS + f1
                    col_im = im_at + which * SUB_BINS + f1
                    band[g * 2 * SUB_BINS + which * SUB_BINS + f1] = f
                else:
                    lane = g * 2 * MORE_BINS + which * MORE_BINS + f1 - SUB_BINS
                    col_re = LANES + lane
                    col_im = LANES + LANES // 2 + lane
                    beyond[lane] = beyond[LANES // 2 + lane] = f
                phase = 2.0 * math.pi / NT * (n0[:, 0] * f % NT)
                cos, sin = np.cos(phase), np.sin(phase)
                if g == 0:
                    rows = slice(which * LANES, (which + 1) * LANES)
                    tables[g, rows, col_re] = cos
                    tables[g, rows, col_im] = -sin
                else:
                    sign = 1.0 if which == 0 else -1.0
                    tables[g, :LANES, col_re] = cos
                    tables[g, LANES:, col_re] = sign * sin
                    tables[g, :LANES, col_im] = -sin
                    tables[g, LANES:, col_im] = sign * cos
    return tables, band, beyond


def constants():
    tables, band, beyond = transform_tables()
    source = np.concatenate([band, beyond])[:, None]
    inside = (np.abs(source - band[None, :]) <= HALF).astype(ml_dtypes.bfloat16)
    count = np.minimum(band + HALF, F - 1) - np.maximum(band - HALF, 0) + 1
    per_bin = (1.0 / count).astype(np.float32)[None, :]
    phase = 2.0 * math.pi / NT * (band[:, None] * (np.arange(LAGS)[None, :] - LAGS // 2 + NT) % NT)
    lags = np.concatenate([np.cos(phase), -np.sin(phase)]).astype(np.float32)
    lags = lags.astype(ml_dtypes.bfloat16).astype(np.float32) / math.sqrt(WINDOWS * FB)
    return band_matrix(), halves(tables), inside, per_bin, lags.astype(ml_dtypes.bfloat16)


def real_dft(x):
    n = len(x)
    if n == 2:
        return [(x[0] + x[1], None), (x[0] - x[1], None)]
    half = n // 2
    even = real_dft([x[b] + x[b + half] for b in range(half)])
    odd = [x[b] - x[b + half] for b in range(half)]
    out = [None] * (half + 1)
    out[::2] = even
    for f in range(1, half, 2):
        re = odd[0]
        im = odd[half // 2] * -math.sin(math.pi * f / 2)
        for b in range(1, half // 2):
            re = re + (odd[b] - odd[half - b]) * math.cos(2 * math.pi * f * b / n)
            im = im - (odd[b] + odd[half - b]) * math.sin(2 * math.pi * f * b / n)
        out[f] = (re, im)
    return out


def split(x):
    high = x.astype(jnp.bfloat16)
    return high, (x - high.astype(jnp.float32)).astype(jnp.bfloat16)


def dot(a, b):
    return jnp.dot(a, b, preferred_element_type=jnp.float32)


def both_halves(x, table_high, table_low):
    rows = x.shape[0]
    high, low = split(x)
    top = dot(jnp.concatenate([high, low], axis=0), table_high)
    return top[:rows] + top[rows:] + dot(high, table_low)


def flip(index, mask, bits):
    for b in range(bits):
        bit = 1 << b
        index = index + (mask // bit % 2) * bit * (1 - 2 * (index // bit % 2))
    return index


def whiten(starts, records, band, tables, inside, per_bin, waits):
    traces = []
    for w in range(WINDOWS):
        start = starts[w]
        last = records.shape[1] - STRIDE * (CHUNKS - 1) - SPAN
        base = jnp.minimum(start // LANES * LANES, last)
        if w == 0:
            waits[0]()
        raw = jnp.concatenate(
            [
                records[:, pl.ds(pl.multiple_of(base + STRIDE * b, LANES), SPAN)]
                for b in range(CHUNKS)
            ],
            axis=0,
        )
        taps_high, taps_low = split(band[pl.ds(RESID - (start - base), SPAN), :])
        traces.append(both_halves(raw, taps_high, taps_low))
    pieces = [
        jnp.concatenate([t[CH * b : CH * (b + 1)] for t in traces], axis=0) for b in range(CHUNKS)
    ]
    bins = real_dft(pieces)
    waits[1]()
    outs = []
    for g in range(GROUPS):
        if g == 0:
            x = jnp.concatenate([bins[0][0], bins[CHUNKS // 2][0]], axis=1)
        else:
            x = jnp.concatenate(bins[g], axis=1)
        outs.append(both_halves(x, tables[0, g], tables[1, g]))
    beyond = functools.reduce(lambda a, b: a + b, [o[:, LANES:] for o in outs])
    first = lax.broadcasted_iota(jnp.int32, (WINDOWS * CH, LANES), 1) < LANES // 2
    re, im = [], []
    for q in range(GROUPS // 2):
        a, b = outs[2 * q][:, :LANES], outs[2 * q + 1][:, :LANES]
        re.append(jnp.where(first, a, b))
        im.append(pltpu.roll(jnp.where(first, b, a), LANES // 2, 1))
    re, im = jnp.concatenate(re, axis=1), jnp.concatenate(im, axis=1)
    power = jnp.concatenate([re * re + im * im, beyond * beyond], axis=1)
    waits[2]()
    both = dot(jnp.concatenate(split(power), axis=0), inside[...])
    smoothed = (both[: WINDOWS * CH] + both[WINDOWS * CH :]) * per_bin[...]
    scale = lax.rsqrt(smoothed + eps_power)
    return jnp.concatenate([re * scale, im * scale], axis=1).astype(jnp.bfloat16)


def spectra_kernel(
    starts, records_hbm, band_hbm, tables_hbm, inside_hbm, per_bin_hbm, out,
    records, band, tables, inside, per_bin, load_sem,
):
    loads = [
        pltpu.make_async_copy(a, b, load_sem.at[i])
        for i, (a, b) in enumerate(
            [(records_hbm, records), (band_hbm, band), (tables_hbm, tables), (inside_hbm, inside),
             (per_bin_hbm, per_bin)]
        )
    ]
    for load in loads:
        load.start()

    def first_wait():
        loads[0].wait()
        loads[1].wait()

    def last_wait():
        loads[3].wait()
        loads[4].wait()

    out[...] = whiten(
        starts, records, band, tables, inside, per_bin, [first_wait, loads[2].wait, last_wait]
    )


def pair_kernel(
    n_src, n_rcv, mask, own, lags_hbm, out,
    lags, src_buf, rcv_buf, src_f32, held_rcv, cross_even, cross_odd, threshold,
    load_sem, src_send, src_recv, rcv_send, rcv_recv,
):
    me_s, me_r = lax.axis_index("src"), lax.axis_index("rcv")
    src_bits, rcv_bits = n_src.bit_length() - 1, n_rcv.bit_length() - 1
    load = pltpu.make_async_copy(lags_hbm, lags, load_sem)
    load.start()

    barrier = pltpu.get_barrier_semaphore()

    def greet_src(k, _):
        peer = flip(me_s, k, src_bits)
        pl.semaphore_signal(barrier, inc=1, device_id={"src": peer}, device_id_type=MESH)
        return 0

    def greet_rcv(k, _):
        peer = flip(me_r, k, rcv_bits)
        pl.semaphore_signal(barrier, inc=1, device_id={"rcv": peer}, device_id_type=MESH)
        return 0

    lax.fori_loop(1, n_src, greet_src, 0)
    lax.fori_loop(1, n_rcv, greet_rcv, 0)

    src_buf[me_s] = own[...]
    rcv_buf[me_r] = own[...]
    pl.semaphore_wait(barrier, n_src + n_rcv - 2)

    def src_copy(slot, peer):
        return pltpu.make_async_remote_copy(
            src_ref=src_buf.at[slot], dst_ref=src_buf.at[slot], send_sem=src_send.at[peer],
            recv_sem=src_recv.at[slot], device_id={"src": peer}, device_id_type=MESH,
        )

    def rcv_copy(slot, peer):
        return pltpu.make_async_remote_copy(
            src_ref=rcv_buf.at[slot], dst_ref=rcv_buf.at[slot], send_sem=rcv_send.at[peer],
            recv_sem=rcv_recv.at[slot], device_id={"rcv": peer}, device_id_type=MESH,
        )

    def send_rcv(k, _):
        peer = flip(me_r, k, rcv_bits)

        @pl.when(peer < me_r)
        def _():
            rcv_copy(me_r, peer).start()

        return 0

    def send_src(k, _):
        src_copy(me_s, flip(me_s, k, src_bits)).start()
        return 0

    lax.fori_loop(1, n_rcv, send_rcv, 0)
    lax.fori_loop(1, n_src, send_src, 0)

    block_rows = n_src * CH
    for b in range(n_rcv):
        ids = lax.broadcasted_iota(jnp.int32, (CH, LAGS), 0) + b * block_rows + me_s * CH
        threshold[CH * b : CH * (b + 1), :] = jnp.where(mask[0, b] > 0, ids, -1)

    load.wait()
    units = n_src // 2
    own_pair = me_r // 2

    def clear(p, _):
        for i in range(n_src * CH):
            out[i, pl.ds(pl.multiple_of(p * PAIR, PAIR), PAIR), :] = jnp.zeros((PAIR, LAGS), out.dtype)
        return 0

    lax.fori_loop(0, own_pair, clear, 0)

    def one_pair(p, _):
        at = pl.ds(pl.multiple_of(p * PAIR, PAIR), PAIR)
        for i in range(2):
            block = 2 * p + i

            @pl.when(block > me_r)
            def _():
                rcv_copy(block, block).wait_recv()

            @pl.when(block < me_r)
            def _():
                rcv_buf[block] = jnp.zeros(rcv_buf.shape[1:], rcv_buf.dtype)

        both = [rcv_buf[2 * p + i].astype(jnp.float32) for i in range(2)]
        for w in range(WINDOWS):
            rows = slice(w * CH, (w + 1) * CH)
            held_rcv[w] = jnp.concatenate([x[rows] for x in both], axis=0).astype(jnp.bfloat16)

        def arrive(u, first):
            for i in range(first, 2):

                @pl.when(p == own_pair)
                def _():
                    peer = flip(me_s, 2 * u + i, src_bits)
                    src_copy(peer, peer).wait_recv()

        def products(u, cross):
            for i in range(2):
                src_f32[i] = src_buf[flip(me_s, 2 * u + i, src_bits)].astype(jnp.float32)
            for q in range(FB // LANES):
                lo, hi = slice(q * LANES, (q + 1) * LANES), slice(FB + q * LANES, FB + (q + 1) * LANES)
                held = [(held_rcv[w, :, lo], held_rcv[w, :, hi]) for w in range(WINDOWS)]
                for c in range(2 * CH):
                    re = im = None
                    for w in range(WINDOWS):
                        row = slice(w * CH + c % CH, w * CH + c % CH + 1)
                        s_re, s_im = [
                            jnp.broadcast_to(src_f32[c // CH, row, x], (PAIR, LANES)).astype(jnp.bfloat16)
                            for x in (lo, hi)
                        ]
                        r_re, r_im = held[w]
                        one = s_re * r_re + s_im * r_im
                        two = s_im * r_re - s_re * r_im
                        re = one if re is None else re + one
                        im = two if im is None else im + two
                    cross[c * PAIR : (c + 1) * PAIR, lo] = re
                    cross[c * PAIR : (c + 1) * PAIR, hi] = im

        def lagged(u, cross):
            values = dot(cross[...], lags[...])
            limit = threshold[at, :]
            for c in range(2 * CH):
                row = flip(me_s, 2 * u + c // CH, src_bits) * CH + c % CH
                keep = limit > me_r * block_rows + row
                value = jnp.where(keep, values[c * PAIR : (c + 1) * PAIR], 0.0)
                out[row, at, :] = value.astype(jnp.bfloat16)

        arrive(0, 1)
        products(0, cross_even)

        def two_units(t, _):
            arrive(2 * t + 1, 0)
            products(2 * t + 1, cross_odd)
            lagged(2 * t, cross_even)
            arrive(2 * t + 2, 0)
            products(2 * t + 2, cross_even)
            lagged(2 * t + 1, cross_odd)
            return 0

        lax.fori_loop(0, units // 2 - 1, two_units, 0)
        arrive(units - 1, 0)
        products(units - 1, cross_odd)
        lagged(units - 2, cross_even)
        lagged(units - 1, cross_odd)
        return 0

    lax.fori_loop(own_pair, n_rcv // 2, one_pair, 0)

    def sent_src(k, _):
        src_copy(me_s, flip(me_s, k, src_bits)).wait_send()
        return 0

    def sent_rcv(k, _):
        rcv_copy(me_r, k).wait_send()
        return 0

    lax.fori_loop(1, n_src, sent_src, 0)
    lax.fori_loop(0, me_r, sent_rcv, 0)


def on_device(n_src, n_rcv, records, starts, block_mask):
    band, tables, inside, per_bin, lags = constants()
    rows = n_rcv * CH
    held = (WINDOWS * CH, 2 * FB)
    smem = pl.BlockSpec(memory_space=pltpu.SMEM)
    vmem = pl.BlockSpec(memory_space=pltpu.VMEM)
    anywhere = pl.BlockSpec(memory_space=pl.ANY)
    own = pl.pallas_call(
        spectra_kernel,
        out_shape=jax.ShapeDtypeStruct(held, jnp.bfloat16),
        in_specs=[smem] + [anywhere] * 5,
        out_specs=vmem,
        scratch_shapes=[
            pltpu.VMEM(records.shape, jnp.float32),
            pltpu.VMEM(band.shape, jnp.float32),
            pltpu.VMEM(tables.shape, jnp.bfloat16),
            pltpu.VMEM(inside.shape, jnp.bfloat16),
            pltpu.VMEM(per_bin.shape, jnp.float32),
            pltpu.SemaphoreType.DMA((5,)),
        ],
        compiler_params=pltpu.CompilerParams(vmem_limit_bytes=60 * 1024 * 1024),
    )(starts, records, band, tables, inside, per_bin)
    result = pl.pallas_call(
        functools.partial(pair_kernel, n_src, n_rcv),
        out_shape=jax.ShapeDtypeStruct((n_src * CH, rows, LAGS), jnp.bfloat16),
        in_specs=[smem, vmem, anywhere],
        out_specs=vmem,
        scratch_shapes=[
            pltpu.VMEM(lags.shape, jnp.bfloat16),
            pltpu.VMEM((n_src,) + held, jnp.bfloat16),
            pltpu.VMEM((n_rcv,) + held, jnp.bfloat16),
            pltpu.VMEM((2,) + held, jnp.float32),
            pltpu.VMEM((WINDOWS, PAIR, 2 * FB), jnp.bfloat16),
            pltpu.VMEM((2 * CH * PAIR, 2 * FB), jnp.bfloat16),
            pltpu.VMEM((2 * CH * PAIR, 2 * FB), jnp.bfloat16),
            pltpu.VMEM((rows, LAGS), jnp.int32),
            pltpu.SemaphoreType.DMA,
            pltpu.SemaphoreType.DMA((n_src,)),
            pltpu.SemaphoreType.DMA((n_src,)),
            pltpu.SemaphoreType.DMA((n_rcv,)),
            pltpu.SemaphoreType.DMA((n_rcv,)),
        ],
        compiler_params=pltpu.CompilerParams(
            collective_id=0, has_side_effects=True, vmem_limit_bytes=24 * 1024 * 1024
        ),
    )(block_mask.reshape(1, n_rcv), own, lags)
    return result.reshape(n_src * CH, n_rcv, 1, CH, LAGS)


def solution(mesh):
    in_specs = (P(("rcv", "src"), None), P(), P("rcv", None, "src"))
    out_specs = P("rcv", None, "src", None, None)
    return jax.shard_map(
        functools.partial(on_device, mesh.shape["src"], mesh.shape["rcv"]),
        mesh=mesh, in_specs=in_specs, out_specs=out_specs, check_vma=False,
    )
```

```python
import functools
import math

import jax
import jax.numpy as jnp
import ml_dtypes
import numpy as np
from jax import lax
from jax.experimental import pallas as pl
from jax.experimental.pallas import tpu as pltpu
from jax.sharding import PartitionSpec as P

DEC = 5
NT = 2048
FB = 512
HALF = 64
LAGS = 128
TAPS = 65
F = 1024
LANES = 128
WINDOWS = 2
CH = 8
PAIR = 2 * CH

CHUNKS = NT // LANES
STRIDE = DEC * LANES
SPAN = 7 * LANES
RESID = 200
SUB_BINS = FB // CHUNKS
MORE_BINS = HALF // CHUNKS
GROUPS = CHUNKS // 2

eps_power = 1e-06
MESH = pl.DeviceIdType.MESH


def residues(group):
    return (0, CHUNKS // 2) if group == 0 else (group, CHUNKS - group)


def halves(table):
    high = table.astype(ml_dtypes.bfloat16)
    low = (table - high.astype(np.float64)).astype(ml_dtypes.bfloat16)
    return np.stack([high, low])


def band_matrix():
    tap = np.arange(TAPS, dtype=np.float64)
    taper = 0.5 - 0.5 * np.cos(2.0 * math.pi * (tap + 1.0) / (TAPS + 1.0))
    taps = np.sinc((tap - (TAPS - 1) / 2.0) / DEC) * taper / DEC
    k = np.arange(SPAN + RESID)[:, None] - RESID - DEC * np.arange(LANES)[None, :]
    return np.where((k >= 0) & (k < TAPS), taps[np.clip(k, 0, TAPS - 1)], 0.0).astype(np.float32)


def transform_tables():
    n0 = np.arange(LANES)[:, None]
    tables = np.zeros((GROUPS, 2 * LANES, 2 * LANES))
    band = np.zeros(FB, np.int64)
    beyond = np.zeros(LANES, np.int64)
    for g in range(GROUPS):
        re_at, im_at = (0, LANES // 2) if g % 2 == 0 else (LANES // 2, 0)
        for which, f0 in enumerate(residues(g)):
            for f1 in range(SUB_BINS + MORE_BINS):
                f = CHUNKS * f1 + f0
                if f1 < SUB_BINS:
                    col_re = re_at + which * SUB_BINS + f1
                    col_im = im_at + which * SUB_BINS + f1
                    band[g * 2 * SUB_BINS + which * SUB_BINS + f1] = f
                else:
                    lane = g * 2 * MORE_BINS + which * MORE_BINS + f1 - SUB_BINS
                    col_re = LANES + lane
                    col_im = LANES + LANES // 2 + lane
                    beyond[lane] = beyond[LANES // 2 + lane] = f
                phase = 2.0 * math.pi / NT * (n0[:, 0] * f % NT)
                cos, sin = np.cos(phase), np.sin(phase)
                if g == 0:
                    rows = slice(which * LANES, (which + 1) * LANES)
                    tables[g, rows, col_re] = cos
                    tables[g, rows, col_im] = -sin
                else:
                    sign = 1.0 if which == 0 else -1.0
                    tables[g, :LANES, col_re] = cos
                    tables[g, LANES:, col_re] = sign * sin
                    tables[g, :LANES, col_im] = -sin
                    tables[g, LANES:, col_im] = sign * cos
    return tables, band, beyond


def constants():
    tables, band, beyond = transform_tables()
    source = np.concatenate([band, beyond])[:, None]
    inside = (np.abs(source - band[None, :]) <= HALF).astype(ml_dtypes.bfloat16)
    count = np.minimum(band + HALF, F - 1) - np.maximum(band - HALF, 0) + 1
    per_bin = (1.0 / count).astype(np.float32)[None, :]
    phase = 2.0 * math.pi / NT * (band[:, None] * (np.arange(LAGS)[None, :] - LAGS // 2 + NT) % NT)
    lags = np.concatenate([np.cos(phase), -np.sin(phase)]).astype(np.float32)
    lags = lags.astype(ml_dtypes.bfloat16).astype(np.float32) / math.sqrt(WINDOWS * FB)
    return band_matrix(), halves(tables), inside, per_bin, lags.astype(ml_dtypes.bfloat16)


def real_dft(x):
    n = len(x)
    if n == 2:
        return [(x[0] + x[1], None), (x[0] - x[1], None)]
    half = n // 2
    even = real_dft([x[b] + x[b + half] for b in range(half)])
    odd = [x[b] - x[b + half] for b in range(half)]
    out = [None] * (half + 1)
    out[::2] = even
    for f in range(1, half, 2):
        re = odd[0]
        im = odd[half // 2] * -math.sin(math.pi * f / 2)
        for b in range(1, half // 2):
            re = re + (odd[b] - odd[half - b]) * math.cos(2 * math.pi * f * b / n)
            im = im - (odd[b] + odd[half - b]) * math.sin(2 * math.pi * f * b / n)
        out[f] = (re, im)
    return out


def split(x):
    high = x.astype(jnp.bfloat16)
    return high, (x - high.astype(jnp.float32)).astype(jnp.bfloat16)


def dot(a, b):
    return jnp.dot(a, b, preferred_element_type=jnp.float32)


def both_halves(x, table_high, table_low):
    rows = x.shape[0]
    high, low = split(x)
    top = dot(jnp.concatenate([high, low], axis=0), table_high)
    return top[:rows] + top[rows:] + dot(high, table_low)


def flip(index, mask, bits):
    for b in range(bits):
        bit = 1 << b
        index = index + (mask // bit % 2) * bit * (1 - 2 * (index // bit % 2))
    return index


def whiten(starts, records, band, tables, inside, per_bin, waits):
    traces = []
    for w in range(WINDOWS):
        start = starts[w]
        last = records.shape[1] - STRIDE * (CHUNKS - 1) - SPAN
        base = jnp.minimum(start // LANES * LANES, last)
        if w == 0:
            waits[0]()
        raw = jnp.concatenate(
            [
                records[:, pl.ds(pl.multiple_of(base + STRIDE * b, LANES), SPAN)]
                for b in range(CHUNKS)
            ],
            axis=0,
        )
        taps_high, taps_low = split(band[pl.ds(RESID - (start - base), SPAN), :])
        traces.append(both_halves(raw, taps_high, taps_low))
    pieces = [
        jnp.concatenate([t[CH * b : CH * (b + 1)] for t in traces], axis=0) for b in range(CHUNKS)
    ]
    bins = real_dft(pieces)
    waits[1]()
    outs = []
    for g in range(GROUPS):
        if g == 0:
            x = jnp.concatenate([bins[0][0], bins[CHUNKS // 2][0]], axis=1)
        else:
            x = jnp.concatenate(bins[g], axis=1)
        outs.append(both_halves(x, tables[0, g], tables[1, g]))
    beyond = functools.reduce(lambda a, b: a + b, [o[:, LANES:] for o in outs])
    first = lax.broadcasted_iota(jnp.int32, (WINDOWS * CH, LANES), 1) < LANES // 2
    re, im = [], []
    for q in range(GROUPS // 2):
        a, b = outs[2 * q][:, :LANES], outs[2 * q + 1][:, :LANES]
        re.append(jnp.where(first, a, b))
        im.append(pltpu.roll(jnp.where(first, b, a), LANES // 2, 1))
    re, im = jnp.concatenate(re, axis=1), jnp.concatenate(im, axis=1)
    power = jnp.concatenate([re * re + im * im, beyond * beyond], axis=1)
    waits[2]()
    both = dot(jnp.concatenate(split(power), axis=0), inside[...])
    smoothed = (both[: WINDOWS * CH] + both[WINDOWS * CH :]) * per_bin[...]
    scale = lax.rsqrt(smoothed + eps_power)
    return jnp.concatenate([re * scale, im * scale], axis=1).astype(jnp.bfloat16)


def spectra_kernel(
    starts, records_hbm, band_hbm, tables_hbm, inside_hbm, per_bin_hbm, out,
    records, band, tables, inside, per_bin, load_sem,
):
    loads = [
        pltpu.make_async_copy(a, b, load_sem.at[i])
        for i, (a, b) in enumerate(
            [(records_hbm, records), (band_hbm, band), (tables_hbm, tables), (inside_hbm, inside),
             (per_bin_hbm, per_bin)]
        )
    ]
    for load in loads:
        load.start()

    def first_wait():
        loads[0].wait()
        loads[1].wait()

    def last_wait():
        loads[3].wait()
        loads[4].wait()

    out[...] = whiten(
        starts, records, band, tables, inside, per_bin, [first_wait, loads[2].wait, last_wait]
    )


def pair_kernel(
    n_src, n_rcv, mask, own, lags_hbm, out,
    lags, src_buf, rcv_buf, held_rcv, cross_even, cross_odd, lag_even, lag_odd, threshold,
    load_sem, src_send, src_recv, rcv_send, rcv_recv,
):
    me_s, me_r = lax.axis_index("src"), lax.axis_index("rcv")
    src_bits, rcv_bits = n_src.bit_length() - 1, n_rcv.bit_length() - 1
    load = pltpu.make_async_copy(lags_hbm, lags, load_sem)
    load.start()

    barrier = pltpu.get_barrier_semaphore()

    def greet_src(k, _):
        peer = flip(me_s, k, src_bits)
        pl.semaphore_signal(barrier, inc=1, device_id={"src": peer}, device_id_type=MESH)
        return 0

    def greet_rcv(k, _):
        peer = flip(me_r, k, rcv_bits)
        pl.semaphore_signal(barrier, inc=1, device_id={"rcv": peer}, device_id_type=MESH)
        return 0

    lax.fori_loop(1, n_src, greet_src, 0)
    lax.fori_loop(1, n_rcv, greet_rcv, 0)

    src_buf[me_s] = own[...]
    rcv_buf[me_r] = own[...]
    pl.semaphore_wait(barrier, n_src + n_rcv - 2)

    def src_copy(slot, peer):
        return pltpu.make_async_remote_copy(
            src_ref=src_buf.at[slot], dst_ref=src_buf.at[slot], send_sem=src_send.at[peer],
            recv_sem=src_recv.at[slot], device_id={"src": peer}, device_id_type=MESH,
        )

    def rcv_copy(slot, peer):
        return pltpu.make_async_remote_copy(
            src_ref=rcv_buf.at[slot], dst_ref=rcv_buf.at[slot], send_sem=rcv_send.at[peer],
            recv_sem=rcv_recv.at[slot], device_id={"rcv": peer}, device_id_type=MESH,
        )

    def send_rcv(k, _):
        peer = flip(me_r, k, rcv_bits)

        @pl.when(peer < me_r)
        def _():
            rcv_copy(me_r, peer).start()

        return 0

    def send_src(k, _):
        src_copy(me_s, flip(me_s, k, src_bits)).start()
        return 0

    lax.fori_loop(1, n_rcv, send_rcv, 0)
    lax.fori_loop(1, n_src, send_src, 0)

    block_rows = n_src * CH
    for b in range(n_rcv):
        ids = lax.broadcasted_iota(jnp.int32, (CH, LAGS), 0) + b * block_rows + me_s * CH
        threshold[CH * b : CH * (b + 1), :] = jnp.where(mask[0, b] > 0, ids, -1)

    load.wait()
    units = n_src // 2
    own_pair = me_r // 2

    def clear(p, _):
        for i in range(n_src * CH):
            out[i, pl.ds(pl.multiple_of(p * PAIR, PAIR), PAIR), :] = jnp.zeros((PAIR, LAGS), out.dtype)
        return 0

    lax.fori_loop(0, own_pair, clear, 0)

    def one_pair(p, _):
        at = pl.ds(pl.multiple_of(p * PAIR, PAIR), PAIR)
        for i in range(2):
            block = 2 * p + i

            @pl.when(block > me_r)
            def _():
                rcv_copy(block, block).wait_recv()

            @pl.when(block < me_r)
            def _():
                rcv_buf[block] = jnp.zeros(rcv_buf.shape[1:], rcv_buf.dtype)

        for i in range(2):
            both = rcv_buf[2 * p + i].astype(jnp.float32)
            for j in range(CH):
                for w in range(WINDOWS):
                    spread = jnp.broadcast_to(both[w * CH + j : w * CH + j + 1], (PAIR, 2 * FB))
                    held_rcv[i * CH + j, w] = spread.astype(jnp.bfloat16)

        def arrive(u, first):
            for i in range(first, 2):

                @pl.when(p == own_pair)
                def _():
                    peer = flip(me_s, 2 * u + i, src_bits)
                    src_copy(peer, peer).wait_recv()

        def products(u, cross):
            both = [src_buf[flip(me_s, 2 * u + i, src_bits)].astype(jnp.float32) for i in range(2)]
            held = [
                jnp.concatenate([x[w * CH : (w + 1) * CH] for x in both], axis=0).astype(jnp.bfloat16)
                for w in range(WINDOWS)
            ]
            for q in range(FB // LANES):
                lo, hi = slice(q * LANES, (q + 1) * LANES), slice(FB + q * LANES, FB + (q + 1) * LANES)
                for j in range(PAIR):
                    re = im = None
                    for w in range(WINDOWS):
                        s_re, s_im = held[w][:, lo], held[w][:, hi]
                        r_re, r_im = held_rcv[j, w, :, lo], held_rcv[j, w, :, hi]
                        one = s_re * r_re + s_im * r_im
                        two = s_im * r_re - s_re * r_im
                        re = one if re is None else re + one
                        im = two if im is None else im + two
                    cross[j * PAIR : (j + 1) * PAIR, lo] = re
                    cross[j * PAIR : (j + 1) * PAIR, hi] = im

        def lagged(u, cross, values):
            values[...] = dot(cross[...], lags[...])
            limit = threshold[at, :]
            for c in range(2 * CH):
                row = flip(me_s, 2 * u + c // CH, src_bits) * CH + c % CH
                keep = limit > me_r * block_rows + row
                value = jnp.where(keep, values[pl.ds(c, PAIR, stride=PAIR), :], 0.0)
                out[row, at, :] = value.astype(jnp.bfloat16)

        arrive(0, 1)
        products(0, cross_even)

        def two_units(t, _):
            arrive(2 * t + 1, 0)
            products(2 * t + 1, cross_odd)
            lagged(2 * t, cross_even, lag_even)
            arrive(2 * t + 2, 0)
            products(2 * t + 2, cross_even)
            lagged(2 * t + 1, cross_odd, lag_odd)
            return 0

        lax.fori_loop(0, units // 2 - 1, two_units, 0)
        arrive(units - 1, 0)
        products(units - 1, cross_odd)
        lagged(units - 2, cross_even, lag_even)
        lagged(units - 1, cross_odd, lag_odd)
        return 0

    lax.fori_loop(own_pair, n_rcv // 2, one_pair, 0)

    def sent_src(k, _):
        src_copy(me_s, flip(me_s, k, src_bits)).wait_send()
        return 0

    def sent_rcv(k, _):
        rcv_copy(me_r, k).wait_send()
        return 0

    lax.fori_loop(1, n_src, sent_src, 0)
    lax.fori_loop(0, me_r, sent_rcv, 0)


def on_device(n_src, n_rcv, records, starts, block_mask):
    band, tables, inside, per_bin, lags = constants()
    rows = n_rcv * CH
    held = (WINDOWS * CH, 2 * FB)
    smem = pl.BlockSpec(memory_space=pltpu.SMEM)
    vmem = pl.BlockSpec(memory_space=pltpu.VMEM)
    anywhere = pl.BlockSpec(memory_space=pl.ANY)
    own = pl.pallas_call(
        spectra_kernel,
        out_shape=jax.ShapeDtypeStruct(held, jnp.bfloat16),
        in_specs=[smem] + [anywhere] * 5,
        out_specs=vmem,
        scratch_shapes=[
            pltpu.VMEM(records.shape, jnp.float32),
            pltpu.VMEM(band.shape, jnp.float32),
            pltpu.VMEM(tables.shape, jnp.bfloat16),
            pltpu.VMEM(inside.shape, jnp.bfloat16),
            pltpu.VMEM(per_bin.shape, jnp.float32),
            pltpu.SemaphoreType.DMA((5,)),
        ],
        compiler_params=pltpu.CompilerParams(vmem_limit_bytes=60 * 1024 * 1024),
    )(starts, records, band, tables, inside, per_bin)
    result = pl.pallas_call(
        functools.partial(pair_kernel, n_src, n_rcv),
        out_shape=jax.ShapeDtypeStruct((n_src * CH, rows, LAGS), jnp.bfloat16),
        in_specs=[smem, vmem, anywhere],
        out_specs=vmem,
        scratch_shapes=[
            pltpu.VMEM(lags.shape, jnp.bfloat16),
            pltpu.VMEM((n_src,) + held, jnp.bfloat16),
            pltpu.VMEM((n_rcv,) + held, jnp.bfloat16),
            pltpu.VMEM((PAIR, WINDOWS, PAIR, 2 * FB), jnp.bfloat16),
            pltpu.VMEM((PAIR * PAIR, 2 * FB), jnp.bfloat16),
            pltpu.VMEM((PAIR * PAIR, 2 * FB), jnp.bfloat16),
            pltpu.VMEM((PAIR * PAIR, LAGS), jnp.float32),
            pltpu.VMEM((PAIR * PAIR, LAGS), jnp.float32),
            pltpu.VMEM((rows, LAGS), jnp.int32),
            pltpu.SemaphoreType.DMA,
            pltpu.SemaphoreType.DMA((n_src,)),
            pltpu.SemaphoreType.DMA((n_src,)),
            pltpu.SemaphoreType.DMA((n_rcv,)),
            pltpu.SemaphoreType.DMA((n_rcv,)),
        ],
        compiler_params=pltpu.CompilerParams(
            collective_id=0, has_side_effects=True, vmem_limit_bytes=24 * 1024 * 1024
        ),
    )(block_mask.reshape(1, n_rcv), own, lags)
    return result.reshape(n_src * CH, n_rcv, 1, CH, LAGS)


def solution(mesh):
    in_specs = (P(("rcv", "src"), None), P(), P("rcv", None, "src"))
    out_specs = P("rcv", None, "src", None, None)
    return jax.shard_map(
        functools.partial(on_device, mesh.shape["src"], mesh.shape["rcv"]),
        mesh=mesh, in_specs=in_specs, out_specs=out_specs, check_vma=False,
    )
```

```python
import functools
import math

import jax
import jax.numpy as jnp
import ml_dtypes
import numpy as np
from jax import lax
from jax.experimental import pallas as pl
from jax.experimental.pallas import tpu as pltpu
from jax.sharding import PartitionSpec as P

DEC = 5
NT = 2048
FB = 512
HALF = 64
LAGS = 128
TAPS = 65
F = 1024
LANES = 128
WINDOWS = 2
CH = 8
PAIR = 2 * CH

CHUNKS = NT // LANES
STRIDE = DEC * LANES
SPAN = 7 * LANES
RESID = 200
SUB_BINS = FB // CHUNKS
MORE_BINS = HALF // CHUNKS
GROUPS = CHUNKS // 2

eps_power = 1e-06
MESH = pl.DeviceIdType.MESH


def residues(group):
    return (0, CHUNKS // 2) if group == 0 else (group, CHUNKS - group)


def halves(table):
    high = table.astype(ml_dtypes.bfloat16)
    low = (table - high.astype(np.float64)).astype(ml_dtypes.bfloat16)
    return np.stack([high, low])


def band_matrix():
    tap = np.arange(TAPS, dtype=np.float64)
    taper = 0.5 - 0.5 * np.cos(2.0 * math.pi * (tap + 1.0) / (TAPS + 1.0))
    taps = np.sinc((tap - (TAPS - 1) / 2.0) / DEC) * taper / DEC
    k = np.arange(SPAN + RESID)[:, None] - RESID - DEC * np.arange(LANES)[None, :]
    return np.where((k >= 0) & (k < TAPS), taps[np.clip(k, 0, TAPS - 1)], 0.0).astype(np.float32)


def transform_tables():
    n0 = np.arange(LANES)[:, None]
    tables = np.zeros((GROUPS, 2 * LANES, 2 * LANES))
    band = np.zeros(FB, np.int64)
    beyond = np.zeros(LANES, np.int64)
    for g in range(GROUPS):
        re_at, im_at = (0, LANES // 2) if g % 2 == 0 else (LANES // 2, 0)
        for which, f0 in enumerate(residues(g)):
            for f1 in range(SUB_BINS + MORE_BINS):
                f = CHUNKS * f1 + f0
                if f1 < SUB_BINS:
                    col_re = re_at + which * SUB_BINS + f1
                    col_im = im_at + which * SUB_BINS + f1
                    band[g * 2 * SUB_BINS + which * SUB_BINS + f1] = f
                else:
                    lane = g * 2 * MORE_BINS + which * MORE_BINS + f1 - SUB_BINS
                    col_re = LANES + lane
                    col_im = LANES + LANES // 2 + lane
                    beyond[lane] = beyond[LANES // 2 + lane] = f
                phase = 2.0 * math.pi / NT * (n0[:, 0] * f % NT)
                cos, sin = np.cos(phase), np.sin(phase)
                if g == 0:
                    rows = slice(which * LANES, (which + 1) * LANES)
                    tables[g, rows, col_re] = cos
                    tables[g, rows, col_im] = -sin
                else:
                    sign = 1.0 if which == 0 else -1.0
                    tables[g, :LANES, col_re] = cos
                    tables[g, LANES:, col_re] = sign * sin
                    tables[g, :LANES, col_im] = -sin
                    tables[g, LANES:, col_im] = sign * cos
    return tables, band, beyond


def constants():
    tables, band, beyond = transform_tables()
    source = np.concatenate([band, beyond])[:, None]
    inside = (np.abs(source - band[None, :]) <= HALF).astype(ml_dtypes.bfloat16)
    count = np.minimum(band + HALF, F - 1) - np.maximum(band - HALF, 0) + 1
    per_bin = (1.0 / count).astype(np.float32)[None, :]
    phase = 2.0 * math.pi / NT * (band[:, None] * (np.arange(LAGS)[None, :] - LAGS // 2 + NT) % NT)
    lags = np.concatenate([np.cos(phase), -np.sin(phase)]).astype(np.float32)
    lags = lags.astype(ml_dtypes.bfloat16).astype(np.float32) / math.sqrt(WINDOWS * FB)
    return band_matrix(), halves(tables), inside, per_bin, lags.astype(ml_dtypes.bfloat16)


def real_dft(x):
    n = len(x)
    if n == 2:
        return [(x[0] + x[1], None), (x[0] - x[1], None)]
    half = n // 2
    even = real_dft([x[b] + x[b + half] for b in range(half)])
    odd = [x[b] - x[b + half] for b in range(half)]
    out = [None] * (half + 1)
    out[::2] = even
    for f in range(1, half, 2):
        re = odd[0]
        im = odd[half // 2] * -math.sin(math.pi * f / 2)
        for b in range(1, half // 2):
            re = re + (odd[b] - odd[half - b]) * math.cos(2 * math.pi * f * b / n)
            im = im - (odd[b] + odd[half - b]) * math.sin(2 * math.pi * f * b / n)
        out[f] = (re, im)
    return out


def split(x):
    high = x.astype(jnp.bfloat16)
    return high, (x - high.astype(jnp.float32)).astype(jnp.bfloat16)


def dot(a, b):
    return jnp.dot(a, b, preferred_element_type=jnp.float32)


def both_halves(x, table_high, table_low):
    rows = x.shape[0]
    high, low = split(x)
    top = dot(jnp.concatenate([high, low], axis=0), table_high)
    return top[:rows] + top[rows:] + dot(high, table_low)


def flip(index, mask, bits):
    for b in range(bits):
        bit = 1 << b
        index = index + (mask // bit % 2) * bit * (1 - 2 * (index // bit % 2))
    return index


def whiten(starts, records, band, tables, inside, per_bin, waits):
    traces = []
    for w in range(WINDOWS):
        start = starts[w]
        last = records.shape[1] - STRIDE * (CHUNKS - 1) - SPAN
        base = jnp.minimum(start // LANES * LANES, last)
        if w == 0:
            waits[0]()
        raw = jnp.concatenate(
            [
                records[:, pl.ds(pl.multiple_of(base + STRIDE * b, LANES), SPAN)]
                for b in range(CHUNKS)
            ],
            axis=0,
        )
        taps_high, taps_low = split(band[pl.ds(RESID - (start - base), SPAN), :])
        traces.append(both_halves(raw, taps_high, taps_low))
    pieces = [
        jnp.concatenate([t[CH * b : CH * (b + 1)] for t in traces], axis=0) for b in range(CHUNKS)
    ]
    bins = real_dft(pieces)
    waits[1]()
    outs = []
    for g in range(GROUPS):
        if g == 0:
            x = jnp.concatenate([bins[0][0], bins[CHUNKS // 2][0]], axis=1)
        else:
            x = jnp.concatenate(bins[g], axis=1)
        outs.append(both_halves(x, tables[0, g], tables[1, g]))
    beyond = functools.reduce(lambda a, b: a + b, [o[:, LANES:] for o in outs])
    first = lax.broadcasted_iota(jnp.int32, (WINDOWS * CH, LANES), 1) < LANES // 2
    re, im = [], []
    for q in range(GROUPS // 2):
        a, b = outs[2 * q][:, :LANES], outs[2 * q + 1][:, :LANES]
        re.append(jnp.where(first, a, b))
        im.append(pltpu.roll(jnp.where(first, b, a), LANES // 2, 1))
    re, im = jnp.concatenate(re, axis=1), jnp.concatenate(im, axis=1)
    power = jnp.concatenate([re * re + im * im, beyond * beyond], axis=1)
    waits[2]()
    both = dot(jnp.concatenate(split(power), axis=0), inside[...])
    smoothed = (both[: WINDOWS * CH] + both[WINDOWS * CH :]) * per_bin[...]
    scale = lax.rsqrt(smoothed + eps_power)
    return jnp.concatenate([re * scale, im * scale], axis=1).astype(jnp.bfloat16)


def spectra_kernel(
    starts, records_hbm, band_hbm, tables_hbm, inside_hbm, per_bin_hbm, out,
    records, band, tables, inside, per_bin, load_sem,
):
    loads = [
        pltpu.make_async_copy(a, b, load_sem.at[i])
        for i, (a, b) in enumerate(
            [(records_hbm, records), (band_hbm, band), (tables_hbm, tables), (inside_hbm, inside),
             (per_bin_hbm, per_bin)]
        )
    ]
    for load in loads:
        load.start()
    def first_wait():
        loads[0].wait()
        loads[1].wait()

    def last_wait():
        loads[3].wait()
        loads[4].wait()

    out[...] = whiten(
        starts, records, band, tables, inside, per_bin, [first_wait, loads[2].wait, last_wait]
    )


def pair_kernel(
    n_src, n_rcv, mask, own, lags_hbm, out,
    lags, src_buf, rcv_buf, src_f32, held_rcv, cross_even, cross_odd, threshold,
    load_sem, own_sem, src_send, fwd_send, src_recv, rcv_send, rcv_recv,
):
    me_s, me_r = lax.axis_index("src"), lax.axis_index("rcv")
    src_bits, rcv_bits = n_src.bit_length() - 1, n_rcv.bit_length() - 1
    load = pltpu.make_async_copy(lags_hbm, lags, load_sem)
    load.start()
    places = [
        pltpu.make_async_copy(own, src_buf.at[me_s], own_sem.at[0]),
        pltpu.make_async_copy(own, rcv_buf.at[me_r], own_sem.at[1]),
    ]
    for place in places:
        place.start()

    barrier = pltpu.get_barrier_semaphore()

    sibling = flip(me_s, 1, src_bits)

    def greet_src(k, _):
        peer = flip(me_s, 2 * k, src_bits)
        pl.semaphore_signal(barrier, inc=1, device_id={"src": peer}, device_id_type=MESH)
        return 0

    def greet_rcv(k, _):
        pl.semaphore_signal(barrier, inc=1, device_id={"rcv": k}, device_id_type=MESH)
        return 0

    pl.semaphore_signal(barrier, inc=1, device_id={"src": sibling}, device_id_type=MESH)
    lax.fori_loop(1, n_src // 2, greet_src, 0)
    lax.fori_loop(me_r + 1, n_rcv, greet_rcv, 0)
    pl.semaphore_wait(barrier, n_src // 2 + me_r)
    for place in places:
        place.wait()

    def src_copy(slot, peer):
        return pltpu.make_async_remote_copy(
            src_ref=src_buf.at[slot], dst_ref=src_buf.at[slot], send_sem=src_send.at[peer],
            recv_sem=src_recv.at[slot], device_id={"src": peer}, device_id_type=MESH,
        )

    def forward(slot):
        return pltpu.make_async_remote_copy(
            src_ref=src_buf.at[slot], dst_ref=src_buf.at[slot], send_sem=fwd_send.at[slot],
            recv_sem=src_recv.at[slot], device_id={"src": sibling}, device_id_type=MESH,
        )

    def rcv_copy(slot, peer):
        return pltpu.make_async_remote_copy(
            src_ref=rcv_buf.at[slot], dst_ref=rcv_buf.at[slot], send_sem=rcv_send.at[peer],
            recv_sem=rcv_recv.at[slot], device_id={"rcv": peer}, device_id_type=MESH,
        )

    def send_rcv(k, _):
        rcv_copy(me_r, me_r - 1 - k).start()
        return 0

    def send_src(k, _):
        src_copy(me_s, flip(me_s, 2 * k, src_bits)).start()
        return 0

    lax.fori_loop(1, n_src // 2, send_src, 0)
    lax.fori_loop(0, me_r, send_rcv, 0)
    src_copy(me_s, sibling).start()

    block_rows = n_src * CH
    for b in range(n_rcv):
        ids = lax.broadcasted_iota(jnp.int32, (CH, LAGS), 0) + b * block_rows + me_s * CH
        threshold[CH * b : CH * (b + 1), :] = jnp.where(mask[0, b] > 0, ids, -1)

    load.wait()
    units = n_src // 2
    own_pair = me_r // 2

    def clear(p, _):
        for i in range(n_src * CH):
            out[i, pl.ds(pl.multiple_of(p * PAIR, PAIR), PAIR), :] = jnp.zeros((PAIR, LAGS), out.dtype)
        return 0

    lax.fori_loop(0, own_pair, clear, 0)

    def one_pair(p, _):
        at = pl.ds(pl.multiple_of(p * PAIR, PAIR), PAIR)
        for i in range(2):
            block = 2 * p + i

            @pl.when(block > me_r)
            def _():
                rcv_copy(block, block).wait_recv()

            @pl.when(block < me_r)
            def _():
                rcv_buf[block] = jnp.zeros(rcv_buf.shape[1:], rcv_buf.dtype)

        both = [rcv_buf[2 * p + i].astype(jnp.float32) for i in range(2)]
        for w in range(WINDOWS):
            rows = slice(w * CH, (w + 1) * CH)
            held_rcv[w] = jnp.concatenate([x[rows] for x in both], axis=0).astype(jnp.bfloat16)

        def land(k):
            peer = flip(me_s, k, src_bits)
            src_copy(peer, peer).wait_recv()
            forward(peer).start()

        def arrive(u):
            first = p == own_pair

            @pl.when(first & (u == 1))
            def _():
                land(2)

            @pl.when(first & (u > 0) & (u < units - 1))
            def _():
                land(2 * u + 2)

            @pl.when(first)
            def _():
                peer = flip(me_s, 2 * u + 1, src_bits)
                src_copy(peer, peer).wait_recv()

        def products(u, cross):
            for i in range(2):
                src_f32[i] = src_buf[flip(me_s, 2 * u + i, src_bits)].astype(jnp.float32)
            for q in range(FB // LANES):
                lo, hi = slice(q * LANES, (q + 1) * LANES), slice(FB + q * LANES, FB + (q + 1) * LANES)
                held = [(held_rcv[w, :, lo], held_rcv[w, :, hi]) for w in range(WINDOWS)]
                for c in range(2 * CH):
                    re = im = None
                    for w in range(WINDOWS):
                        row = slice(w * CH + c % CH, w * CH + c % CH + 1)
                        s_re, s_im = [
                            jnp.broadcast_to(src_f32[c // CH, row, x], (PAIR, LANES)).astype(jnp.bfloat16)
                            for x in (lo, hi)
                        ]
                        r_re, r_im = held[w]
                        one = s_re * r_re + s_im * r_im
                        two = s_im * r_re - s_re * r_im
                        re = one if re is None else re + one
                        im = two if im is None else im + two
                    cross[c * PAIR : (c + 1) * PAIR, lo] = re
                    cross[c * PAIR : (c + 1) * PAIR, hi] = im

        def lagged(u, cross):
            values = dot(cross[...], lags[...])
            limit = threshold[at, :]
            for c in range(2 * CH):
                row = flip(me_s, 2 * u + c // CH, src_bits) * CH + c % CH
                keep = limit > me_r * block_rows + row
                value = jnp.where(keep, values[c * PAIR : (c + 1) * PAIR], 0.0)
                out[row, at, :] = value.astype(jnp.bfloat16)

        arrive(0)
        products(0, cross_even)

        def two_units(t, _):
            arrive(2 * t + 1)
            products(2 * t + 1, cross_odd)
            lagged(2 * t, cross_even)
            arrive(2 * t + 2)
            products(2 * t + 2, cross_even)
            lagged(2 * t + 1, cross_odd)
            return 0

        lax.fori_loop(0, units // 2 - 1, two_units, 0)
        arrive(units - 1)
        products(units - 1, cross_odd)
        lagged(units - 2, cross_even)
        lagged(units - 1, cross_odd)
        return 0

    lax.fori_loop(own_pair, n_rcv // 2, one_pair, 0)

    def sent_src(k, _):
        peer = flip(me_s, 2 * k, src_bits)
        src_copy(me_s, peer).wait_send()
        forward(peer).wait_send()
        return 0

    def sent_rcv(k, _):
        rcv_copy(me_r, k).wait_send()
        return 0

    src_copy(me_s, sibling).wait_send()
    lax.fori_loop(1, n_src // 2, sent_src, 0)
    lax.fori_loop(0, me_r, sent_rcv, 0)


def on_device(n_src, n_rcv, records, starts, block_mask):
    band, tables, inside, per_bin, lags = constants()
    rows = n_rcv * CH
    held = (WINDOWS * CH, 2 * FB)
    smem = pl.BlockSpec(memory_space=pltpu.SMEM)
    vmem = pl.BlockSpec(memory_space=pltpu.VMEM)
    anywhere = pl.BlockSpec(memory_space=pl.ANY)
    own = pl.pallas_call(
        spectra_kernel,
        out_shape=jax.ShapeDtypeStruct(held, jnp.bfloat16),
        in_specs=[smem] + [anywhere] * 5,
        out_specs=vmem,
        scratch_shapes=[
            pltpu.VMEM(records.shape, jnp.float32),
            pltpu.VMEM(band.shape, jnp.float32),
            pltpu.VMEM(tables.shape, jnp.bfloat16),
            pltpu.VMEM(inside.shape, jnp.bfloat16),
            pltpu.VMEM(per_bin.shape, jnp.float32),
            pltpu.SemaphoreType.DMA((5,)),
        ],
        compiler_params=pltpu.CompilerParams(vmem_limit_bytes=60 * 1024 * 1024),
    )(starts, records, band, tables, inside, per_bin)
    result = pl.pallas_call(
        functools.partial(pair_kernel, n_src, n_rcv),
        out_shape=jax.ShapeDtypeStruct((n_src * CH, rows, LAGS), jnp.bfloat16),
        in_specs=[smem, anywhere, anywhere],
        out_specs=vmem,
        scratch_shapes=[
            pltpu.VMEM(lags.shape, jnp.bfloat16),
            pltpu.VMEM((n_src,) + held, jnp.bfloat16),
            pltpu.VMEM((n_rcv,) + held, jnp.bfloat16),
            pltpu.VMEM((2,) + held, jnp.float32),
            pltpu.VMEM((WINDOWS, PAIR, 2 * FB), jnp.bfloat16),
            pltpu.VMEM((2 * CH * PAIR, 2 * FB), jnp.bfloat16),
            pltpu.VMEM((2 * CH * PAIR, 2 * FB), jnp.bfloat16),
            pltpu.VMEM((rows, LAGS), jnp.int32),
            pltpu.SemaphoreType.DMA,
            pltpu.SemaphoreType.DMA((2,)),
            pltpu.SemaphoreType.DMA((n_src,)),
            pltpu.SemaphoreType.DMA((n_src,)),
            pltpu.SemaphoreType.DMA((n_src,)),
            pltpu.SemaphoreType.DMA((n_rcv,)),
            pltpu.SemaphoreType.DMA((n_rcv,)),
        ],
        compiler_params=pltpu.CompilerParams(
            collective_id=0, has_side_effects=True, vmem_limit_bytes=24 * 1024 * 1024
        ),
    )(block_mask.reshape(1, n_rcv), own, lags)
    return result.reshape(n_src * CH, n_rcv, 1, CH, LAGS)


def solution(mesh):
    in_specs = (P(("rcv", "src"), None), P(), P("rcv", None, "src"))
    out_specs = P("rcv", None, "src", None, None)
    return jax.shard_map(
        functools.partial(on_device, mesh.shape["src"], mesh.shape["rcv"]),
        mesh=mesh, in_specs=in_specs, out_specs=out_specs, check_vma=False,
    )
```

```python
import functools
import math

import jax
import jax.numpy as jnp
import ml_dtypes
import numpy as np
from jax import lax
from jax.experimental import pallas as pl
from jax.experimental.pallas import tpu as pltpu
from jax.sharding import PartitionSpec as P

DEC = 5
NT = 2048
FB = 512
HALF = 64
LAGS = 128
TAPS = 65
F = 1024
LANES = 128
WINDOWS = 2
CH = 8
PAIR = 2 * CH

CHUNKS = NT // LANES
STRIDE = DEC * LANES
SPAN = 7 * LANES
RESID = 200
SUB_BINS = FB // CHUNKS
MORE_BINS = HALF // CHUNKS
GROUPS = CHUNKS // 2

eps_power = 1e-06
MESH = pl.DeviceIdType.MESH


def residues(group):
    return (0, CHUNKS // 2) if group == 0 else (group, CHUNKS - group)


def halves(table):
    high = table.astype(ml_dtypes.bfloat16)
    low = (table - high.astype(np.float64)).astype(ml_dtypes.bfloat16)
    return np.stack([high, low])


def band_matrix():
    tap = np.arange(TAPS, dtype=np.float64)
    taper = 0.5 - 0.5 * np.cos(2.0 * math.pi * (tap + 1.0) / (TAPS + 1.0))
    taps = np.sinc((tap - (TAPS - 1) / 2.0) / DEC) * taper / DEC
    k = np.arange(SPAN + RESID)[:, None] - RESID - DEC * np.arange(LANES)[None, :]
    return np.where((k >= 0) & (k < TAPS), taps[np.clip(k, 0, TAPS - 1)], 0.0).astype(np.float32)


def transform_tables():
    n0 = np.arange(LANES)[:, None]
    tables = np.zeros((GROUPS, 2 * LANES, 2 * LANES))
    band = np.zeros(FB, np.int64)
    beyond = np.zeros(LANES, np.int64)
    for g in range(GROUPS):
        re_at, im_at = (0, LANES // 2) if g % 2 == 0 else (LANES // 2, 0)
        for which, f0 in enumerate(residues(g)):
            for f1 in range(SUB_BINS + MORE_BINS):
                f = CHUNKS * f1 + f0
                if f1 < SUB_BINS:
                    col_re = re_at + which * SUB_BINS + f1
                    col_im = im_at + which * SUB_BINS + f1
                    band[g * 2 * SUB_BINS + which * SUB_BINS + f1] = f
                else:
                    lane = g * 2 * MORE_BINS + which * MORE_BINS + f1 - SUB_BINS
                    col_re = LANES + lane
                    col_im = LANES + LANES // 2 + lane
                    beyond[lane] = beyond[LANES // 2 + lane] = f
                phase = 2.0 * math.pi / NT * (n0[:, 0] * f % NT)
                cos, sin = np.cos(phase), np.sin(phase)
                if g == 0:
                    rows = slice(which * LANES, (which + 1) * LANES)
                    tables[g, rows, col_re] = cos
                    tables[g, rows, col_im] = -sin
                else:
                    sign = 1.0 if which == 0 else -1.0
                    tables[g, :LANES, col_re] = cos
                    tables[g, LANES:, col_re] = sign * sin
                    tables[g, :LANES, col_im] = -sin
                    tables[g, LANES:, col_im] = sign * cos
    return tables, band, beyond


def constants():
    tables, band, beyond = transform_tables()
    source = np.concatenate([band, beyond])[:, None]
    inside = (np.abs(source - band[None, :]) <= HALF).astype(ml_dtypes.bfloat16)
    count = np.minimum(band + HALF, F - 1) - np.maximum(band - HALF, 0) + 1
    per_bin = (1.0 / count).astype(np.float32)[None, :]
    phase = 2.0 * math.pi / NT * (band[:, None] * (np.arange(LAGS)[None, :] - LAGS // 2 + NT) % NT)
    lags = np.concatenate([np.cos(phase), -np.sin(phase)]).astype(np.float32)
    lags = lags.astype(ml_dtypes.bfloat16).astype(np.float32) / math.sqrt(WINDOWS * FB)
    return band_matrix(), halves(tables), inside, per_bin, lags.astype(ml_dtypes.bfloat16)


def real_dft(x):
    n = len(x)
    if n == 2:
        return [(x[0] + x[1], None), (x[0] - x[1], None)]
    half = n // 2
    even = real_dft([x[b] + x[b + half] for b in range(half)])
    odd = [x[b] - x[b + half] for b in range(half)]
    out = [None] * (half + 1)
    out[::2] = even
    for f in range(1, half, 2):
        re = odd[0]
        im = odd[half // 2] * -math.sin(math.pi * f / 2)
        for b in range(1, half // 2):
            re = re + (odd[b] - odd[half - b]) * math.cos(2 * math.pi * f * b / n)
            im = im - (odd[b] + odd[half - b]) * math.sin(2 * math.pi * f * b / n)
        out[f] = (re, im)
    return out


def split(x):
    high = x.astype(jnp.bfloat16)
    return high, (x - high.astype(jnp.float32)).astype(jnp.bfloat16)


def dot(a, b):
    return jnp.dot(a, b, preferred_element_type=jnp.float32)


def both_halves(x, table_high, table_low):
    rows = x.shape[0]
    high, low = split(x)
    top = dot(jnp.concatenate([high, low], axis=0), table_high)
    return top[:rows] + top[rows:] + dot(high, table_low)


def flip(index, mask, bits):
    for b in range(bits):
        bit = 1 << b
        index = index + (mask // bit % 2) * bit * (1 - 2 * (index // bit % 2))
    return index


def whiten(starts, records, band, tables, inside, per_bin, waits):
    traces = []
    for w in range(WINDOWS):
        start = starts[w]
        last = records.shape[1] - STRIDE * (CHUNKS - 1) - SPAN
        base = jnp.minimum(start // LANES * LANES, last)
        if w == 0:
            waits[0]()
        raw = jnp.concatenate(
            [
                records[:, pl.ds(pl.multiple_of(base + STRIDE * b, LANES), SPAN)]
                for b in range(CHUNKS)
            ],
            axis=0,
        )
        taps_high, taps_low = split(band[pl.ds(RESID - (start - base), SPAN), :])
        traces.append(both_halves(raw, taps_high, taps_low))
    pieces = [
        jnp.concatenate([t[CH * b : CH * (b + 1)] for t in traces], axis=0) for b in range(CHUNKS)
    ]
    bins = real_dft(pieces)
    waits[1]()
    outs = []
    for g in range(GROUPS):
        if g == 0:
            x = jnp.concatenate([bins[0][0], bins[CHUNKS // 2][0]], axis=1)
        else:
            x = jnp.concatenate(bins[g], axis=1)
        outs.append(both_halves(x, tables[0, g], tables[1, g]))
    beyond = functools.reduce(lambda a, b: a + b, [o[:, LANES:] for o in outs])
    first = lax.broadcasted_iota(jnp.int32, (WINDOWS * CH, LANES), 1) < LANES // 2
    re, im = [], []
    for q in range(GROUPS // 2):
        a, b = outs[2 * q][:, :LANES], outs[2 * q + 1][:, :LANES]
        re.append(jnp.where(first, a, b))
        im.append(pltpu.roll(jnp.where(first, b, a), LANES // 2, 1))
    re, im = jnp.concatenate(re, axis=1), jnp.concatenate(im, axis=1)
    power = jnp.concatenate([re * re + im * im, beyond * beyond], axis=1)
    waits[2]()
    both = dot(jnp.concatenate(split(power), axis=0), inside[...])
    smoothed = (both[: WINDOWS * CH] + both[WINDOWS * CH :]) * per_bin[...]
    scale = lax.rsqrt(smoothed + eps_power)
    return jnp.concatenate([re * scale, im * scale], axis=1).astype(jnp.bfloat16)


def spectra_kernel(
    starts, records_hbm, band_hbm, tables_hbm, inside_hbm, per_bin_hbm, out,
    records, band, tables, inside, per_bin, load_sem,
):
    loads = [
        pltpu.make_async_copy(a, b, load_sem.at[i])
        for i, (a, b) in enumerate(
            [(records_hbm, records), (band_hbm, band), (tables_hbm, tables), (inside_hbm, inside),
             (per_bin_hbm, per_bin)]
        )
    ]
    for load in loads:
        load.start()
    def first_wait():
        loads[0].wait()
        loads[1].wait()

    def last_wait():
        loads[3].wait()
        loads[4].wait()

    out[...] = whiten(
        starts, records, band, tables, inside, per_bin, [first_wait, loads[2].wait, last_wait]
    )


def pair_kernel(
    n_src, n_rcv, mask, own, lags_hbm, out,
    lags, src_buf, rcv_buf, src_f32, held_rcv, cross_even, cross_odd, threshold,
    load_sem, own_sem, src_send, fwd_send, src_recv, rcv_send, rcv_recv,
):
    me_s, me_r = lax.axis_index("src"), lax.axis_index("rcv")
    src_bits, rcv_bits = n_src.bit_length() - 1, n_rcv.bit_length() - 1
    load = pltpu.make_async_copy(lags_hbm, lags, load_sem)
    load.start()
    places = [
        pltpu.make_async_copy(own, src_buf.at[me_s], own_sem.at[0]),
        pltpu.make_async_copy(own, rcv_buf.at[me_r], own_sem.at[1]),
    ]
    for place in places:
        place.start()

    barrier = pltpu.get_barrier_semaphore()

    sibling = flip(me_s, 1, src_bits)

    def greet_src(k, _):
        peer = flip(me_s, 2 * k, src_bits)
        pl.semaphore_signal(barrier, inc=1, device_id={"src": peer}, device_id_type=MESH)
        return 0

    def greet_rcv(k, _):
        pl.semaphore_signal(barrier, inc=1, device_id={"rcv": k}, device_id_type=MESH)
        return 0

    pl.semaphore_signal(barrier, inc=1, device_id={"src": sibling}, device_id_type=MESH)
    lax.fori_loop(1, n_src // 2, greet_src, 0)
    lax.fori_loop(me_r + 1, n_rcv, greet_rcv, 0)
    pl.semaphore_wait(barrier, n_src // 2 + me_r)
    for place in places:
        place.wait()

    def src_copy(slot, peer):
        return pltpu.make_async_remote_copy(
            src_ref=src_buf.at[slot], dst_ref=src_buf.at[slot], send_sem=src_send.at[peer],
            recv_sem=src_recv.at[slot], device_id={"src": peer}, device_id_type=MESH,
        )

    def forward(slot):
        return pltpu.make_async_remote_copy(
            src_ref=src_buf.at[slot], dst_ref=src_buf.at[slot], send_sem=fwd_send.at[slot],
            recv_sem=src_recv.at[slot], device_id={"src": sibling}, device_id_type=MESH,
        )

    def rcv_copy(slot, peer):
        return pltpu.make_async_remote_copy(
            src_ref=rcv_buf.at[slot], dst_ref=rcv_buf.at[slot], send_sem=rcv_send.at[peer],
            recv_sem=rcv_recv.at[slot], device_id={"rcv": peer}, device_id_type=MESH,
        )

    def send_rcv(k, _):
        rcv_copy(me_r, me_r - 1 - k).start()
        return 0

    def send_src(k, _):
        src_copy(me_s, flip(me_s, 2 * k, src_bits)).start()
        return 0

    lax.fori_loop(1, n_src // 2, send_src, 0)
    lax.fori_loop(0, me_r, send_rcv, 0)
    src_copy(me_s, sibling).start()

    block_rows = n_src * CH
    for b in range(n_rcv):
        ids = lax.broadcasted_iota(jnp.int32, (CH, LAGS), 0) + b * block_rows + me_s * CH
        threshold[CH * b : CH * (b + 1), :] = jnp.where(mask[0, b] > 0, ids, -1)

    load.wait()
    units = n_src // 2
    own_pair = me_r // 2

    def clear(p, _):
        for i in range(n_src * CH):
            out[i, pl.ds(pl.multiple_of(p * PAIR, PAIR), PAIR), :] = jnp.zeros((PAIR, LAGS), out.dtype)
        return 0

    lax.fori_loop(0, own_pair, clear, 0)

    def one_pair(p, _):
        at = pl.ds(pl.multiple_of(p * PAIR, PAIR), PAIR)
        for i in range(2):
            block = 2 * p + i

            @pl.when(block > me_r)
            def _():
                rcv_copy(block, block).wait_recv()

            @pl.when(block < me_r)
            def _():
                rcv_buf[block] = jnp.zeros(rcv_buf.shape[1:], rcv_buf.dtype)

        both = [rcv_buf[2 * p + i].astype(jnp.float32) for i in range(2)]
        for w in range(WINDOWS):
            rows = slice(w * CH, (w + 1) * CH)
            held_rcv[w] = jnp.concatenate([x[rows] for x in both], axis=0).astype(jnp.bfloat16)

        def land(k):
            peer = flip(me_s, k, src_bits)
            src_copy(peer, peer).wait_recv()
            forward(peer).start()

        def arrive(u):
            first = p == own_pair

            @pl.when(first & (u == 1))
            def _():
                land(2)

            @pl.when(first & (u > 0) & (u < units - 1))
            def _():
                land(2 * u + 2)

            @pl.when(first)
            def _():
                peer = flip(me_s, 2 * u + 1, src_bits)
                src_copy(peer, peer).wait_recv()

        def products(u, cross):
            for i in range(2):
                src_f32[i] = src_buf[flip(me_s, 2 * u + i, src_bits)].astype(jnp.float32)
            for q in range(FB // LANES):
                lo, hi = slice(q * LANES, (q + 1) * LANES), slice(FB + q * LANES, FB + (q + 1) * LANES)
                held = [(held_rcv[w, :, lo], held_rcv[w, :, hi]) for w in range(WINDOWS)]
                for c in range(2 * CH):
                    re = im = None
                    for w in range(WINDOWS):
                        row = slice(w * CH + c % CH, w * CH + c % CH + 1)
                        s_re, s_im = [
                            jnp.broadcast_to(src_f32[c // CH, row, x], (PAIR, LANES)).astype(jnp.bfloat16)
                            for x in (lo, hi)
                        ]
                        r_re, r_im = held[w]
                        one = s_re * r_re + s_im * r_im
                        two = s_im * r_re - s_re * r_im
                        re = one if re is None else re + one
                        im = two if im is None else im + two
                    cross[c * PAIR : (c + 1) * PAIR, lo] = re
                    cross[c * PAIR : (c + 1) * PAIR, hi] = im

        def lagged(u, cross):
            values = dot(cross[...], lags[...])
            limit = threshold[at, :]
            for c in range(2 * CH):
                row = flip(me_s, 2 * u + c // CH, src_bits) * CH + c % CH
                keep = limit > me_r * block_rows + row
                value = jnp.where(keep, values[c * PAIR : (c + 1) * PAIR], 0.0)
                out[row, at, :] = value.astype(jnp.bfloat16)

        arrive(0)
        products(0, cross_even)

        def two_units(t, _):
            arrive(2 * t + 1)
            products(2 * t + 1, cross_odd)
            lagged(2 * t, cross_even)
            arrive(2 * t + 2)
            products(2 * t + 2, cross_even)
            lagged(2 * t + 1, cross_odd)
            return 0

        lax.fori_loop(0, units // 2 - 1, two_units, 0)
        arrive(units - 1)
        products(units - 1, cross_odd)
        lagged(units - 2, cross_even)
        lagged(units - 1, cross_odd)
        return 0

    lax.fori_loop(own_pair, n_rcv // 2, one_pair, 0)

    def sent_src(k, _):
        peer = flip(me_s, 2 * k, src_bits)
        src_copy(me_s, peer).wait_send()
        forward(peer).wait_send()
        return 0

    def sent_rcv(k, _):
        rcv_copy(me_r, k).wait_send()
        return 0

    src_copy(me_s, sibling).wait_send()
    lax.fori_loop(1, n_src // 2, sent_src, 0)
    lax.fori_loop(0, me_r, sent_rcv, 0)


def on_device(n_src, n_rcv, records, starts, block_mask):
    band, tables, inside, per_bin, lags = constants()
    rows = n_rcv * CH
    held = (WINDOWS * CH, 2 * FB)
    smem = pl.BlockSpec(memory_space=pltpu.SMEM)
    vmem = pl.BlockSpec(memory_space=pltpu.VMEM)
    anywhere = pl.BlockSpec(memory_space=pl.ANY)
    own = pl.pallas_call(
        spectra_kernel,
        out_shape=pltpu.VMEM(held, jnp.bfloat16),
        in_specs=[smem] + [anywhere] * 5,
        out_specs=vmem,
        scratch_shapes=[
            pltpu.VMEM(records.shape, jnp.float32),
            pltpu.VMEM(band.shape, jnp.float32),
            pltpu.VMEM(tables.shape, jnp.bfloat16),
            pltpu.VMEM(inside.shape, jnp.bfloat16),
            pltpu.VMEM(per_bin.shape, jnp.float32),
            pltpu.SemaphoreType.DMA((5,)),
        ],
        compiler_params=pltpu.CompilerParams(vmem_limit_bytes=60 * 1024 * 1024),
    )(starts, records, band, tables, inside, per_bin)
    result = pl.pallas_call(
        functools.partial(pair_kernel, n_src, n_rcv),
        out_shape=jax.ShapeDtypeStruct((n_src * CH, rows, LAGS), jnp.bfloat16),
        in_specs=[smem, anywhere, anywhere],
        out_specs=vmem,
        scratch_shapes=[
            pltpu.VMEM(lags.shape, jnp.bfloat16),
            pltpu.VMEM((n_src,) + held, jnp.bfloat16),
            pltpu.VMEM((n_rcv,) + held, jnp.bfloat16),
            pltpu.VMEM((2,) + held, jnp.float32),
            pltpu.VMEM((WINDOWS, PAIR, 2 * FB), jnp.bfloat16),
            pltpu.VMEM((2 * CH * PAIR, 2 * FB), jnp.bfloat16),
            pltpu.VMEM((2 * CH * PAIR, 2 * FB), jnp.bfloat16),
            pltpu.VMEM((rows, LAGS), jnp.int32),
            pltpu.SemaphoreType.DMA,
            pltpu.SemaphoreType.DMA((2,)),
            pltpu.SemaphoreType.DMA((n_src,)),
            pltpu.SemaphoreType.DMA((n_src,)),
            pltpu.SemaphoreType.DMA((n_src,)),
            pltpu.SemaphoreType.DMA((n_rcv,)),
            pltpu.SemaphoreType.DMA((n_rcv,)),
        ],
        compiler_params=pltpu.CompilerParams(
            collective_id=0, has_side_effects=True, vmem_limit_bytes=24 * 1024 * 1024
        ),
    )(block_mask.reshape(1, n_rcv), own, lags)
    return result.reshape(n_src * CH, n_rcv, 1, CH, LAGS)


def solution(mesh):
    in_specs = (P(("rcv", "src"), None), P(), P("rcv", None, "src"))
    out_specs = P("rcv", None, "src", None, None)
    return jax.shard_map(
        functools.partial(on_device, mesh.shape["src"], mesh.shape["rcv"]),
        mesh=mesh, in_specs=in_specs, out_specs=out_specs, check_vma=False,
    )
```

```python
import functools
import math

import jax
import jax.numpy as jnp
import ml_dtypes
import numpy as np
from jax import lax
from jax.experimental import pallas as pl
from jax.experimental.pallas import tpu as pltpu
from jax.sharding import PartitionSpec as P

DEC = 5
NT = 2048
FB = 512
HALF = 64
LAGS = 128
TAPS = 65
F = 1024
LANES = 128
WINDOWS = 2
CH = 8
PAIR = 2 * CH

CHUNKS = NT // LANES
STRIDE = DEC * LANES
SPAN = 7 * LANES
RESID = 200
SUB_BINS = FB // CHUNKS
MORE_BINS = HALF // CHUNKS
GROUPS = CHUNKS // 2

eps_power = 1e-06
MESH = pl.DeviceIdType.MESH


def residues(group):
    return (0, CHUNKS // 2) if group == 0 else (group, CHUNKS - group)


def halves(table):
    high = table.astype(ml_dtypes.bfloat16)
    low = (table - high.astype(np.float64)).astype(ml_dtypes.bfloat16)
    return np.stack([high, low])


def band_matrix():
    tap = np.arange(TAPS, dtype=np.float64)
    taper = 0.5 - 0.5 * np.cos(2.0 * math.pi * (tap + 1.0) / (TAPS + 1.0))
    taps = np.sinc((tap - (TAPS - 1) / 2.0) / DEC) * taper / DEC
    k = np.arange(SPAN + RESID)[:, None] - RESID - DEC * np.arange(LANES)[None, :]
    return np.where((k >= 0) & (k < TAPS), taps[np.clip(k, 0, TAPS - 1)], 0.0).astype(np.float32)


def transform_tables():
    n0 = np.arange(LANES)[:, None]
    tables = np.zeros((GROUPS, 2 * LANES, 2 * LANES))
    band = np.zeros(FB, np.int64)
    beyond = np.zeros(LANES, np.int64)
    for g in range(GROUPS):
        re_at, im_at = (0, LANES // 2) if g % 2 == 0 else (LANES // 2, 0)
        for which, f0 in enumerate(residues(g)):
            for f1 in range(SUB_BINS + MORE_BINS):
                f = CHUNKS * f1 + f0
                if f1 < SUB_BINS:
                    col_re = re_at + which * SUB_BINS + f1
                    col_im = im_at + which * SUB_BINS + f1
                    band[g * 2 * SUB_BINS + which * SUB_BINS + f1] = f
                else:
                    lane = g * 2 * MORE_BINS + which * MORE_BINS + f1 - SUB_BINS
                    col_re = LANES + lane
                    col_im = LANES + LANES // 2 + lane
                    beyond[lane] = beyond[LANES // 2 + lane] = f
                phase = 2.0 * math.pi / NT * (n0[:, 0] * f % NT)
                cos, sin = np.cos(phase), np.sin(phase)
                if g == 0:
                    rows = slice(which * LANES, (which + 1) * LANES)
                    tables[g, rows, col_re] = cos
                    tables[g, rows, col_im] = -sin
                else:
                    sign = 1.0 if which == 0 else -1.0
                    tables[g, :LANES, col_re] = cos
                    tables[g, LANES:, col_re] = sign * sin
                    tables[g, :LANES, col_im] = -sin
                    tables[g, LANES:, col_im] = sign * cos
    return tables, band, beyond


def constants():
    tables, band, beyond = transform_tables()
    source = np.concatenate([band, beyond])[:, None]
    inside = (np.abs(source - band[None, :]) <= HALF).astype(ml_dtypes.bfloat16)
    count = np.minimum(band + HALF, F - 1) - np.maximum(band - HALF, 0) + 1
    per_bin = (1.0 / count).astype(np.float32)[None, :]
    phase = 2.0 * math.pi / NT * (band[:, None] * (np.arange(LAGS)[None, :] - LAGS // 2 + NT) % NT)
    lags = np.concatenate([np.cos(phase), -np.sin(phase)]).astype(np.float32)
    lags = lags.astype(ml_dtypes.bfloat16).astype(np.float32) / math.sqrt(WINDOWS * FB)
    return band_matrix(), halves(tables), inside, per_bin, lags.astype(ml_dtypes.bfloat16)


def real_dft(x):
    n = len(x)
    if n == 2:
        return [(x[0] + x[1], None), (x[0] - x[1], None)]
    half = n // 2
    even = real_dft([x[b] + x[b + half] for b in range(half)])
    odd = [x[b] - x[b + half] for b in range(half)]
    out = [None] * (half + 1)
    out[::2] = even
    for f in range(1, half, 2):
        re = odd[0]
        im = odd[half // 2] * -math.sin(math.pi * f / 2)
        for b in range(1, half // 2):
            re = re + (odd[b] - odd[half - b]) * math.cos(2 * math.pi * f * b / n)
            im = im - (odd[b] + odd[half - b]) * math.sin(2 * math.pi * f * b / n)
        out[f] = (re, im)
    return out


def split(x):
    high = x.astype(jnp.bfloat16)
    return high, (x - high.astype(jnp.float32)).astype(jnp.bfloat16)


def dot(a, b):
    return jnp.dot(a, b, preferred_element_type=jnp.float32)


def both_halves(x, table_high, table_low):
    rows = x.shape[0]
    high, low = split(x)
    top = dot(jnp.concatenate([high, low], axis=0), table_high)
    return top[:rows] + top[rows:] + dot(high, table_low)


def flip(index, mask, bits):
    for b in range(bits):
        bit = 1 << b
        index = index + (mask // bit % 2) * bit * (1 - 2 * (index // bit % 2))
    return index


def whiten(starts, records, band, tables, inside, per_bin, waits):
    traces = []
    for w in range(WINDOWS):
        start = starts[w]
        last = records.shape[1] - STRIDE * (CHUNKS - 1) - SPAN
        base = jnp.minimum(start // LANES * LANES, last)
        if w == 0:
            waits[0]()
        raw = jnp.concatenate(
            [
                records[:, pl.ds(pl.multiple_of(base + STRIDE * b, LANES), SPAN)]
                for b in range(CHUNKS)
            ],
            axis=0,
        )
        taps_high, taps_low = split(band[pl.ds(RESID - (start - base), SPAN), :])
        traces.append(both_halves(raw, taps_high, taps_low))
    pieces = [
        jnp.concatenate([t[CH * b : CH * (b + 1)] for t in traces], axis=0) for b in range(CHUNKS)
    ]
    bins = real_dft(pieces)
    waits[1]()
    outs = []
    for g in range(GROUPS):
        if g == 0:
            x = jnp.concatenate([bins[0][0], bins[CHUNKS // 2][0]], axis=1)
        else:
            x = jnp.concatenate(bins[g], axis=1)
        outs.append(both_halves(x, tables[0, g], tables[1, g]))
    beyond = functools.reduce(lambda a, b: a + b, [o[:, LANES:] for o in outs])
    first = lax.broadcasted_iota(jnp.int32, (WINDOWS * CH, LANES), 1) < LANES // 2
    re, im = [], []
    for q in range(GROUPS // 2):
        a, b = outs[2 * q][:, :LANES], outs[2 * q + 1][:, :LANES]
        re.append(jnp.where(first, a, b))
        im.append(pltpu.roll(jnp.where(first, b, a), LANES // 2, 1))
    re, im = jnp.concatenate(re, axis=1), jnp.concatenate(im, axis=1)
    power = jnp.concatenate([re * re + im * im, beyond * beyond], axis=1)
    waits[2]()
    both = dot(jnp.concatenate(split(power), axis=0), inside[...])
    smoothed = (both[: WINDOWS * CH] + both[WINDOWS * CH :]) * per_bin[...]
    scale = lax.rsqrt(smoothed + eps_power)
    return jnp.concatenate([re * scale, im * scale], axis=1).astype(jnp.bfloat16)


def spectra_kernel(
    starts, records_hbm, band_hbm, tables_hbm, inside_hbm, per_bin_hbm, out,
    records, band, tables, inside, per_bin, load_sem,
):
    loads = [
        pltpu.make_async_copy(a, b, load_sem.at[i])
        for i, (a, b) in enumerate(
            [(records_hbm, records), (band_hbm, band), (tables_hbm, tables), (inside_hbm, inside),
             (per_bin_hbm, per_bin)]
        )
    ]
    for load in loads:
        load.start()
    def first_wait():
        loads[0].wait()
        loads[1].wait()

    def last_wait():
        loads[3].wait()
        loads[4].wait()

    out[...] = whiten(
        starts, records, band, tables, inside, per_bin, [first_wait, loads[2].wait, last_wait]
    )


def pair_kernel(
    n_src, n_rcv, mask, own, lags_hbm, out,
    lags, src_buf, rcv_buf, src_f32, held_rcv, cross_even, cross_odd, threshold,
    load_sem, own_sem, src_send, fwd_send, src_recv, rcv_send, rcv_recv,
):
    me_s, me_r = lax.axis_index("src"), lax.axis_index("rcv")
    src_bits, rcv_bits = n_src.bit_length() - 1, n_rcv.bit_length() - 1
    load = pltpu.make_async_copy(lags_hbm, lags, load_sem)
    load.start()
    places = [
        pltpu.make_async_copy(own, src_buf.at[me_s], own_sem.at[0]),
        pltpu.make_async_copy(own, rcv_buf.at[me_r], own_sem.at[1]),
    ]
    for place in places:
        place.start()

    barrier = pltpu.get_barrier_semaphore()

    sibling = flip(me_s, 1, src_bits)

    def greet_src(k, _):
        peer = flip(me_s, 2 * k, src_bits)
        pl.semaphore_signal(barrier, inc=1, device_id={"src": peer}, device_id_type=MESH)
        return 0

    def greet_rcv(k, _):
        pl.semaphore_signal(barrier, inc=1, device_id={"rcv": k}, device_id_type=MESH)
        return 0

    pl.semaphore_signal(barrier, inc=1, device_id={"src": sibling}, device_id_type=MESH)
    lax.fori_loop(1, n_src // 2, greet_src, 0)
    lax.fori_loop(me_r + 1, n_rcv, greet_rcv, 0)
    pl.semaphore_wait(barrier, n_src // 2 + me_r)
    for place in places:
        place.wait()

    def src_copy(slot, peer):
        return pltpu.make_async_remote_copy(
            src_ref=src_buf.at[slot], dst_ref=src_buf.at[slot], send_sem=src_send.at[peer],
            recv_sem=src_recv.at[slot], device_id={"src": peer}, device_id_type=MESH,
        )

    def forward(slot):
        return pltpu.make_async_remote_copy(
            src_ref=src_buf.at[slot], dst_ref=src_buf.at[slot], send_sem=fwd_send.at[slot],
            recv_sem=src_recv.at[slot], device_id={"src": sibling}, device_id_type=MESH,
        )

    def rcv_copy(slot, peer):
        return pltpu.make_async_remote_copy(
            src_ref=rcv_buf.at[slot], dst_ref=rcv_buf.at[slot], send_sem=rcv_send.at[peer],
            recv_sem=rcv_recv.at[slot], device_id={"rcv": peer}, device_id_type=MESH,
        )

    def send_rcv(k, _):
        rcv_copy(me_r, k).start()
        return 0

    def send_src(k, _):
        src_copy(me_s, flip(me_s, 2 * k, src_bits)).start()
        return 0

    lax.fori_loop(0, me_r, send_rcv, 0)
    lax.fori_loop(1, n_src // 2, send_src, 0)
    src_copy(me_s, sibling).start()

    block_rows = n_src * CH
    for b in range(n_rcv):
        ids = lax.broadcasted_iota(jnp.int32, (CH, LAGS), 0) + b * block_rows + me_s * CH
        threshold[CH * b : CH * (b + 1), :] = jnp.where(mask[0, b] > 0, ids, -1)

    load.wait()
    units = n_src // 2
    own_pair = me_r // 2

    def clear(p, _):
        for i in range(n_src * CH):
            out[i, pl.ds(pl.multiple_of(p * PAIR, PAIR), PAIR), :] = jnp.zeros((PAIR, LAGS), out.dtype)
        return 0

    lax.fori_loop(0, own_pair, clear, 0)

    def one_pair(p, _):
        at = pl.ds(pl.multiple_of(p * PAIR, PAIR), PAIR)
        for i in range(2):
            block = 2 * p + i

            @pl.when(block > me_r)
            def _():
                rcv_copy(block, block).wait_recv()

            @pl.when(block < me_r)
            def _():
                rcv_buf[block] = jnp.zeros(rcv_buf.shape[1:], rcv_buf.dtype)

        both = [rcv_buf[2 * p + i].astype(jnp.float32) for i in range(2)]
        for w in range(WINDOWS):
            rows = slice(w * CH, (w + 1) * CH)
            held_rcv[w] = jnp.concatenate([x[rows] for x in both], axis=0).astype(jnp.bfloat16)

        def land(k):
            peer = flip(me_s, k, src_bits)
            src_copy(peer, peer).wait_recv()
            forward(peer).start()

        def arrive(u):
            first = p == own_pair

            @pl.when(first & (u == 1))
            def _():
                land(2)

            @pl.when(first & (u > 0) & (u < units - 1))
            def _():
                land(2 * u + 2)

            @pl.when(first)
            def _():
                peer = flip(me_s, 2 * u + 1, src_bits)
                src_copy(peer, peer).wait_recv()

        def products(u, cross):
            for i in range(2):
                src_f32[i] = src_buf[flip(me_s, 2 * u + i, src_bits)].astype(jnp.float32)
            for q in range(FB // LANES):
                lo, hi = slice(q * LANES, (q + 1) * LANES), slice(FB + q * LANES, FB + (q + 1) * LANES)
                held = [(held_rcv[w, :, lo], held_rcv[w, :, hi]) for w in range(WINDOWS)]
                for c in range(2 * CH):
                    re = im = None
                    for w in range(WINDOWS):
                        row = slice(w * CH + c % CH, w * CH + c % CH + 1)
                        s_re, s_im = [
                            jnp.broadcast_to(src_f32[c // CH, row, x], (PAIR, LANES)).astype(jnp.bfloat16)
                            for x in (lo, hi)
                        ]
                        r_re, r_im = held[w]
                        one = s_re * r_re + s_im * r_im
                        two = s_im * r_re - s_re * r_im
                        re = one if re is None else re + one
                        im = two if im is None else im + two
                    cross[c * PAIR : (c + 1) * PAIR, lo] = re
                    cross[c * PAIR : (c + 1) * PAIR, hi] = im

        def lagged(u, cross):
            values = dot(cross[...], lags[...])
            limit = threshold[at, :]
            for c in range(2 * CH):
                row = flip(me_s, 2 * u + c // CH, src_bits) * CH + c % CH
                keep = limit > me_r * block_rows + row
                value = jnp.where(keep, values[c * PAIR : (c + 1) * PAIR], 0.0)
                out[row, at, :] = value.astype(jnp.bfloat16)

        arrive(0)
        products(0, cross_even)

        def two_units(t, _):
            arrive(2 * t + 1)
            products(2 * t + 1, cross_odd)
            lagged(2 * t, cross_even)
            arrive(2 * t + 2)
            products(2 * t + 2, cross_even)
            lagged(2 * t + 1, cross_odd)
            return 0

        lax.fori_loop(0, units // 2 - 1, two_units, 0)
        arrive(units - 1)
        products(units - 1, cross_odd)
        lagged(units - 2, cross_even)
        lagged(units - 1, cross_odd)
        return 0

    lax.fori_loop(own_pair, n_rcv // 2, one_pair, 0)

    def sent_src(k, _):
        peer = flip(me_s, 2 * k, src_bits)
        src_copy(me_s, peer).wait_send()
        forward(peer).wait_send()
        return 0

    def sent_rcv(k, _):
        rcv_copy(me_r, k).wait_send()
        return 0

    src_copy(me_s, sibling).wait_send()
    lax.fori_loop(1, n_src // 2, sent_src, 0)
    lax.fori_loop(0, me_r, sent_rcv, 0)


def on_device(n_src, n_rcv, records, starts, block_mask):
    band, tables, inside, per_bin, lags = constants()
    rows = n_rcv * CH
    held = (WINDOWS * CH, 2 * FB)
    smem = pl.BlockSpec(memory_space=pltpu.SMEM)
    vmem = pl.BlockSpec(memory_space=pltpu.VMEM)
    anywhere = pl.BlockSpec(memory_space=pl.ANY)
    own = pl.pallas_call(
        spectra_kernel,
        out_shape=pltpu.VMEM(held, jnp.bfloat16),
        in_specs=[smem] + [anywhere] * 5,
        out_specs=vmem,
        scratch_shapes=[
            pltpu.VMEM(records.shape, jnp.float32),
            pltpu.VMEM(band.shape, jnp.float32),
            pltpu.VMEM(tables.shape, jnp.bfloat16),
            pltpu.VMEM(inside.shape, jnp.bfloat16),
            pltpu.VMEM(per_bin.shape, jnp.float32),
            pltpu.SemaphoreType.DMA((5,)),
        ],
        compiler_params=pltpu.CompilerParams(vmem_limit_bytes=60 * 1024 * 1024),
    )(starts, records, band, tables, inside, per_bin)
    result = pl.pallas_call(
        functools.partial(pair_kernel, n_src, n_rcv),
        out_shape=jax.ShapeDtypeStruct((n_src * CH, rows, LAGS), jnp.bfloat16),
        in_specs=[smem, anywhere, anywhere],
        out_specs=vmem,
        scratch_shapes=[
            pltpu.VMEM(lags.shape, jnp.bfloat16),
            pltpu.VMEM((n_src,) + held, jnp.bfloat16),
            pltpu.VMEM((n_rcv,) + held, jnp.bfloat16),
            pltpu.VMEM((2,) + held, jnp.float32),
            pltpu.VMEM((WINDOWS, PAIR, 2 * FB), jnp.bfloat16),
            pltpu.VMEM((2 * CH * PAIR, 2 * FB), jnp.bfloat16),
            pltpu.VMEM((2 * CH * PAIR, 2 * FB), jnp.bfloat16),
            pltpu.VMEM((rows, LAGS), jnp.int32),
            pltpu.SemaphoreType.DMA,
            pltpu.SemaphoreType.DMA((2,)),
            pltpu.SemaphoreType.DMA((n_src,)),
            pltpu.SemaphoreType.DMA((n_src,)),
            pltpu.SemaphoreType.DMA((n_src,)),
            pltpu.SemaphoreType.DMA((n_rcv,)),
            pltpu.SemaphoreType.DMA((n_rcv,)),
        ],
        compiler_params=pltpu.CompilerParams(
            collective_id=0, has_side_effects=True, vmem_limit_bytes=24 * 1024 * 1024
        ),
    )(block_mask.reshape(1, n_rcv), own, lags)
    return result.reshape(n_src * CH, n_rcv, 1, CH, LAGS)


def solution(mesh):
    in_specs = (P(("rcv", "src"), None), P(), P("rcv", None, "src"))
    out_specs = P("rcv", None, "src", None, None)
    return jax.shard_map(
        functools.partial(on_device, mesh.shape["src"], mesh.shape["rcv"]),
        mesh=mesh, in_specs=in_specs, out_specs=out_specs, check_vma=False,
    )
```
